32 devices in a mesh: dp: 16 (over z, y, x), mp: 2 (over core).
Axes of the slice: x: 2, y: 2, z: 4, core: 2. Of those that a mesh axis runs over, the one named last changes fastest.
Arguments:
- tokens: bfloat16 [2, 96, 160, 768], P(None, ('dp', 'mp')), may hold values from -6 to 6
- lengths: int32 [2, 96], P(None, ('dp', 'mp')), may hold values from 95 to 160, as said below
- cotangent: bfloat16 [2, 96, 160, 768], P(None, ('dp', 'mp')), may hold values from -6 to 6
- attn_in: float32 [768, 3, 768], P('dp', None, 'mp')
- attn_out: float32 [768, 768], P('mp', 'dp')
- ffn_in: float32 [768, 3072], P('dp', 'mp')
- ffn_out: float32 [3072, 768], P('mp', 'dp')
- attn_in_first: float32 [768, 3, 768], P('dp', None, 'mp'), may hold values from -32 to 32
- attn_in_second: float32 [768, 3, 768], P('dp', None, 'mp'), may hold values from 2.7648 to 11.0592
- attn_out_first: float32 [768, 768], P('mp', 'dp'), may hold values from -56 to 56
- attn_out_second: float32 [768, 768], P('mp', 'dp'), may hold values from 7.68 to 30.72
- ffn_in_first: float32 [768, 3072], P('dp', 'mp'), may hold values from -56 to 56
- ffn_in_second: float32 [768, 3072], P('dp', 'mp'), may hold values from 7.68 to 30.72
- ffn_out_first: float32 [3072, 768], P('mp', 'dp'), may hold values from -64 to 64
- ffn_out_second: float32 [3072, 768], P('mp', 'dp'), may hold values from 11.0592 to 44.2368
- small: float32 [12, 768], replicated
- small_first: float32 [12, 768], replicated, may hold values from -56 to 56
- small_second: float32 [12, 768], replicated, may hold values from 7.68 to 30.72
Outputs:
- output: bfloat16 [2, 96, 160, 768], P(None, ('dp', 'mp'))
- tokens_grad: float32 [2, 96, 160, 768], P(None, ('dp', 'mp'))
- attn_in_grad: float32 [768, 3, 768], P('dp', None, 'mp')
- attn_in_first_new: float32 [768, 3, 768], P('dp', None, 'mp')
- attn_in_second_new: float32 [768, 3, 768], P('dp', None, 'mp')
- attn_in_new: float32 [768, 3, 768], P('dp', None, 'mp')
- attn_in_low: bfloat16 [768, 3, 768], P('dp', None, 'mp')
- attn_out_grad: float32 [768, 768], P('mp', 'dp')
- attn_out_first_new: float32 [768, 768], P('mp', 'dp')
- attn_out_second_new: float32 [768, 768], P('mp', 'dp')
- attn_out_new: float32 [768, 768], P('mp', 'dp')
- attn_out_low: bfloat16 [768, 768], P('mp', 'dp')
- ffn_in_grad: float32 [768, 3072], P('dp', 'mp')
- ffn_in_first_new: float32 [768, 3072], P('dp', 'mp')
- ffn_in_second_new: float32 [768, 3072], P('dp', 'mp')
- ffn_in_new: float32 [768, 3072], P('dp', 'mp')
- ffn_in_low: bfloat16 [768, 3072], P('dp', 'mp')
- ffn_out_grad: float32 [3072, 768], P('mp', 'dp')
- ffn_out_first_new: float32 [3072, 768], P('mp', 'dp')
- ffn_out_second_new: float32 [3072, 768], P('mp', 'dp')
- ffn_out_new: float32 [3072, 768], P('mp', 'dp')
- ffn_out_low: bfloat16 [3072, 768], P('mp', 'dp')
- small_grad: float32 [12, 768], replicated
- small_first_new: float32 [12, 768], replicated
- small_second_new: float32 [12, 768], replicated
- small_new: float32 [12, 768], replicated
- norms: float32 [2, 4], replicated
The draws below stay inside these ranges and needn't reach their ends.
Inputs may be any that keep to these rules, and one draw needn't show every extreme that they name: `lengths`: true length of each chain; positions at or beyond it are padding; both ends of the range occur in every draw.
All inputs are finite; a program needn't handle non-finite values.
Results may differ from the reference program's by a relative error of at most 0.015.
The reference program's roundings to bfloat16 on the way count: a program that leaves them out, or rounds other values in their place, can miss the bound.
Values may be sent and summed in bfloat16 or wider, within the bound.
A program may use at most 192 MiB of HBM per device.

```python
import math
import jax
import jax.numpy as jnp
from jax import lax

D = 768
HEADS = 12
HEAD = 64
FF = 3072
LEN = 160
MICRO = 2
STEP = 10
CHAINS = 96
NVEC = 12


def ramped(sample, axis):
    extent = sample.shape[axis]
    ramp = 0.5 + jnp.arange(extent, dtype=jnp.float32) / extent
    layout = [1] * sample.ndim
    layout[axis] = extent
    return sample * ramp.reshape(layout)


def draw_lengths(key, part):
    key = jax.random.fold_in(key, 1)
    lowest = LEN * 19 // 32
    drawn = jax.random.randint(key, (MICRO, CHAINS), lowest, LEN + 1, dtype=jnp.int32)
    longest = jax.random.randint(jax.random.fold_in(key, 7), (), 0, CHAINS, dtype=jnp.int32)
    shortest = jax.random.randint(jax.random.fold_in(key, 8), (), 0, CHAINS, dtype=jnp.int32)
    drawn = drawn.at[0, longest].set(LEN)
    return drawn.at[1, shortest].set(lowest)


def draw_attn_in(key, part):
    key = jax.random.fold_in(key, 2)
    layout = (D, 3, D)
    sample = jax.random.normal(key, layout, jnp.float32)
    return ramped(sample, 0) * D ** (-0.5)


def draw_attn_out(key, part):
    key = jax.random.fold_in(key, 3)
    layout = (D, D)
    sample = jax.random.normal(key, layout, jnp.float32)
    return ramped(sample, 1) * (D // 32) ** (-0.5)


def draw_ffn_in(key, part):
    key = jax.random.fold_in(key, 4)
    layout = (D, FF)
    sample = jax.random.normal(key, layout, jnp.float32)
    return ramped(sample, 0) * D ** (-0.5)


def draw_ffn_out(key, part):
    key = jax.random.fold_in(key, 5)
    layout = (FF, D)
    sample = jax.random.normal(key, layout, jnp.float32)
    return ramped(sample, 1) * FF ** (-0.5)


def draw_small(key, part):
    key = jax.random.fold_in(key, 6)
    layout = (NVEC, D)
    sample = jax.random.normal(key, layout, jnp.float32) * 0.5
    factor = jax.random.uniform(jax.random.fold_in(key, 3), layout, jnp.float32, 0.8, 1.2)
    gains = ramped(factor, 1)
    row_index = jnp.arange(NVEC, dtype=jnp.int32)[:, None]
    is_gain = (row_index == 3) | (row_index == 6)
    return jnp.where(is_gain, gains, sample)


def steps_of(own_key, dims, shards, least, largest):
    factor_of, own = 1.0, jax.random.fold_in(own_key, 6)
    for dim, blocks in shards:
        draws = jnp.exp(jax.random.uniform(jax.random.fold_in(own, dim), (blocks,), jnp.float32, least / len(shards), largest / len(shards)))
        factor_of = factor_of * jnp.repeat(draws, dims[dim] // blocks).reshape([-1 if axis == dim else 1 for axis in range(len(dims))])
    return factor_of


def centred(stream_key, dims, deviation, bound, split=(), kind=jnp.bfloat16):
    array = deviation * jax.random.normal(stream_key, dims, jnp.float32)
    if split:
        array = array * steps_of(stream_key, dims, split, -0.22, 0.18)
    return jnp.clip(array, -bound, bound).astype(kind)


def setup_inputs(seed: int = 0) -> dict:
    splits = jax.random.split(jax.random.key(seed), 19)
    tokens = centred(splits[0], (MICRO, CHAINS, LEN, D), 1.0, 6.0, ((1, 32),))
    lengths = draw_lengths(jax.random.fold_in(splits[18], 71), 0)
    cotangent = centred(splits[2], (MICRO, CHAINS, LEN, D), 1.0, 6.0, ((1, 32),))
    attn_in = draw_attn_in(jax.random.fold_in(splits[18], 71), 0)
    attn_out = draw_attn_out(jax.random.fold_in(splits[18], 71), 0)
    ffn_in = draw_ffn_in(jax.random.fold_in(splits[18], 71), 0)
    ffn_out = draw_ffn_out(jax.random.fold_in(splits[18], 71), 0)
    attn_in_first = centred(splits[7], (D, 3, D), (0.11 * 0.3 * (MICRO * CHAINS * LEN) ** 0.5), 32.0, ((0, 16), (2, 2)), jnp.float32)
    attn_in_second = jnp.clip(jnp.exp(math.log(11.0592) - 1.3862944 * jax.random.uniform(splits[8], (D, 3, D), jnp.float32) ** steps_of(splits[8], (D, 3, D), ((0, 16), (2, 2)), -0.2, 0.2)), 2.7648, 11.0592)
    attn_out_first = centred(splits[9], (D, D), (0.11 * 0.5 * (MICRO * CHAINS * LEN) ** 0.5), 56.0, ((0, 2), (1, 16)), jnp.float32)
    attn_out_second = jnp.clip(jnp.exp(math.log(30.72) - 1.3862944 * jax.random.uniform(splits[10], (D, D), jnp.float32) ** steps_of(splits[10], (D, D), ((0, 2), (1, 16)), -0.2, 0.2)), 7.68, 30.72)
    ffn_in_first = centred(splits[11], (D, FF), (0.11 * 0.5 * (MICRO * CHAINS * LEN) ** 0.5), 56.0, ((0, 16), (1, 2)), jnp.float32)
    ffn_in_second = jnp.clip(jnp.exp(math.log(30.72) - 1.3862944 * jax.random.uniform(splits[12], (D, FF), jnp.float32) ** steps_of(splits[12], (D, FF), ((0, 16), (1, 2)), -0.2, 0.2)), 7.68, 30.72)
    ffn_out_first = centred(splits[13], (FF, D), (0.11 * 0.6 * (MICRO * CHAINS * LEN) ** 0.5), 64.0, ((0, 2), (1, 16)), jnp.float32)
    ffn_out_second = jnp.clip(jnp.exp(math.log(44.2368) - 1.3862944 * jax.random.uniform(splits[14], (FF, D), jnp.float32) ** steps_of(splits[14], (FF, D), ((0, 2), (1, 16)), -0.2, 0.2)), 11.0592, 44.2368)
    small = draw_small(jax.random.fold_in(splits[18], 71), 0)
    small_first = centred(splits[16], (NVEC, D), (0.11 * 0.5 * (MICRO * CHAINS * LEN) ** 0.5), 56.0, (), jnp.float32)
    small_second = jnp.clip(jnp.exp(jax.random.uniform(splits[17], (NVEC, D), jnp.float32, math.log(7.68), math.log(30.72))), 7.68, 30.72)
    return dict(tokens=tokens, lengths=lengths, cotangent=cotangent, attn_in=attn_in, attn_out=attn_out, ffn_in=ffn_in, ffn_out=ffn_out, attn_in_first=attn_in_first, attn_in_second=attn_in_second, attn_out_first=attn_out_first, attn_out_second=attn_out_second, ffn_in_first=ffn_in_first, ffn_in_second=ffn_in_second, ffn_out_first=ffn_out_first, ffn_out_second=ffn_out_second, small=small, small_first=small_first, small_second=small_second)


@jax.custom_vjp
def low(v):
    return lax.optimization_barrier(v.astype(jnp.bfloat16)).astype(jnp.float32)

@jax.custom_vjp
def low_back(v):
    return v

def low_keep(v):
    return (low(v), None)

def low_pass(kept, grad):
    return (grad,)

def back_keep(v):
    return (v, None)

def back_low(kept, grad):
    return (low(grad),)
low.defvjp(low_keep, low_pass)
low_back.defvjp(back_keep, back_low)
NORM_EPS = 1e-05
RATE_MATRIX = 0.3
RATE_VECTOR = 0.2
BETA_FIRST = 0.9
BETA_SECOND = 0.999
ADAM_EPS = 1e-06
DECAY_RATE = 0.01
MASKED_SCORE = -1000000000.0

def highest(form, left, right):
    return jnp.einsum(form, left, right, precision=lax.Precision.HIGHEST)

def both_round(values):
    return low(low_back(values))

def layer_norm(hidden, gain, shift):
    center = hidden - lax.optimization_barrier(jnp.mean(hidden, axis=-1, keepdims=True))
    spread = lax.optimization_barrier(jnp.mean(center * center, axis=-1, keepdims=True))
    return center * lax.rsqrt(spread + NORM_EPS) * gain + shift

def attend_chain(pieces):
    queries, key_rows, value_rows, token_mask = pieces
    queries = queries.reshape(LEN, HEADS, HEAD)
    key_rows = key_rows.reshape(LEN, HEADS, HEAD)
    value_rows = value_rows.reshape(LEN, HEADS, HEAD)
    scores = low_back(highest('lhe,she->hls', queries, key_rows) * HEAD ** (-0.5))
    scores = jnp.where(token_mask[None, None, :], scores, MASKED_SCORE)
    probs_low = low(jax.nn.softmax(scores, axis=-1))
    return highest('hls,she->lhe', probs_low, value_rows).reshape(LEN, D)

def forward(inputs, attn_in, attn_out, ffn_in, ffn_out, small, token_mask):
    attn_in = low(attn_in)
    attn_out = low(attn_out)
    ffn_in = low(ffn_in)
    ffn_out = low(ffn_out)
    packed = highest('mcld,dke->mclke', inputs, attn_in)
    queries = both_round(packed[..., 0, :] + small[0])
    key_rows = both_round(packed[..., 1, :])
    value_rows = both_round(packed[..., 2, :] + small[1])
    context = lax.map(jax.checkpoint(attend_chain), (queries.reshape((-1, LEN, D)), key_rows.reshape((-1, LEN, D)), value_rows.reshape((-1, LEN, D)), token_mask.reshape((-1, LEN))))
    context = both_round(context).reshape(inputs.shape)
    attn_branch = low_back(highest('mcld,de->mcle', context, attn_out) + small[2])
    first_out = layer_norm(inputs + attn_branch, small[3], small[4])
    upper = low_back(highest('mcld,df->mclf', low(first_out), ffn_in) + small[8:].reshape(FF))
    hidden = low(jax.nn.gelu(upper, approximate=False))
    down_out = low_back(highest('mclf,fd->mcld', hidden, ffn_out) + small[5])
    return layer_norm(first_out + down_out, small[6], small[7])

def adam_moments(gradient, first_moment, second_moment):
    first_new = BETA_FIRST * first_moment + (1.0 - BETA_FIRST) * gradient
    second_new = BETA_SECOND * second_moment + (1.0 - BETA_SECOND) * gradient * gradient
    direction = first_new / (1.0 - BETA_FIRST ** STEP) / (jnp.sqrt(second_new / (1.0 - BETA_SECOND ** STEP)) + ADAM_EPS)
    return (first_new, second_new, direction)

def lamb_matrix(weight, gradient, first_moment, second_moment):
    first_new, second_new, direction = adam_moments(gradient, first_moment, second_moment)
    direction = direction + DECAY_RATE * weight
    weight_norm = jnp.sqrt(jnp.sum(weight * weight))
    step_norm = jnp.sqrt(jnp.sum(direction * direction))
    renewed = weight - RATE_MATRIX * (weight_norm / step_norm) * direction
    return (first_new, second_new, renewed, renewed.astype(jnp.bfloat16), weight_norm, step_norm)

def reference(tokens, lengths, cotangent, attn_in, attn_out, ffn_in, ffn_out, attn_in_first, attn_in_second, attn_out_first, attn_out_second, ffn_in_first, ffn_in_second, ffn_out_first, ffn_out_second, small, small_first, small_second):
    token_mask = jnp.arange(LEN, dtype=jnp.int32)[None, None, :] < lengths[:, :, None]
    inputs = tokens.astype(jnp.float32)

    def whole_layer(inputs, attn_in, attn_out, ffn_in, ffn_out, small):
        return forward(inputs, attn_in, attn_out, ffn_in, ffn_out, small, token_mask)
    output, pullback = jax.vjp(whole_layer, inputs, attn_in, attn_out, ffn_in, ffn_out, small)
    grads_all = pullback(cotangent.astype(jnp.float32))
    in_first, in_second, in_new, in_low, in_wnorm, in_snorm = lamb_matrix(attn_in, grads_all[1], attn_in_first, attn_in_second)
    mid_first, mid_second, mid_new, mid_low, mid_wnorm, mid_snorm = lamb_matrix(attn_out, grads_all[2], attn_out_first, attn_out_second)
    up_first, up_second, up_new, up_low, up_wnorm, up_snorm = lamb_matrix(ffn_in, grads_all[3], ffn_in_first, ffn_in_second)
    down_first, down_second, down_new, down_low, down_wnorm, down_snorm = lamb_matrix(ffn_out, grads_all[4], ffn_out_first, ffn_out_second)
    small_first_new, small_second_new, small_direction = adam_moments(grads_all[5], small_first, small_second)
    small_new = small - RATE_VECTOR * small_direction
    norms = jnp.stack((jnp.stack((in_wnorm, mid_wnorm, up_wnorm, down_wnorm)), jnp.stack((in_snorm, mid_snorm, up_snorm, down_snorm))))
    return (output.astype(jnp.bfloat16), grads_all[0], grads_all[1], in_first, in_second, in_new, in_low, grads_all[2], mid_first, mid_second, mid_new, mid_low, grads_all[3], up_first, up_second, up_new, up_low, grads_all[4], down_first, down_second, down_new, down_low, grads_all[5], small_first_new, small_second_new, small_new, norms)
```

```python
import functools

import jax
import jax.numpy as jnp
from jax import lax
from jax.experimental import pallas as pl
from jax.experimental.pallas import tpu as pltpu
from jax.sharding import PartitionSpec as P

HEAD = 64
STEP = 10
NORM_EPS = 1e-05
RATE_MATRIX = 0.3
RATE_VECTOR = 0.2
BETA_FIRST = 0.9
BETA_SECOND = 0.999
ADAM_EPS = 1e-06
DECAY_RATE = 0.01
MASKED_SCORE = -1000000000.0

MESH = pl.DeviceIdType.MESH
bf16, f32 = jnp.bfloat16, jnp.float32
UNITS = 12
HALF = 384
WIDE = 768
LANES = 128
QUAD = 256
BLOCK = 32
ROWS = 320


def nn(left, right):
    return lax.dot_general(left, right, (((1,), (0,)), ((), ())), preferred_element_type=f32)


def nt(left, right):
    return lax.dot_general(left, right, (((1,), (1,)), ((), ())), preferred_element_type=f32)


def tn(left, right):
    return lax.dot_general(left, right, (((0,), (0,)), ((), ())), preferred_element_type=f32)


def tile(index, size):
    return pl.ds(pl.multiple_of(index * size, size), size)


def loop(count, body):
    def step(index, carry):
        body(index)
        return carry

    lax.fori_loop(0, count, step, 0)


def mean_last(values):
    return jnp.sum(values, axis=-1, keepdims=True) * (1.0 / values.shape[-1])


def fold_rows(values):
    return jnp.sum(values.reshape(values.shape[0] // 8, 8, values.shape[1]), axis=0)


def head_lane():
    return lax.broadcasted_iota(jnp.int32, (1, QUAD), 1) // HEAD


def spread_heads(values):
    lane = head_lane()
    zero = jnp.zeros_like(values)
    return jnp.concatenate([jnp.where(lane == head, values, zero) for head in range(4)], axis=0)


def pick_heads(values, length):
    lane = head_lane()
    result = values[:length]
    for head in range(1, 4):
        result = jnp.where(lane == head, values[head * length : (head + 1) * length], result)
    return result


def pair(ref, rows, offset):
    return jnp.concatenate(
        [ref[rows, pl.ds(offset, LANES)], ref[rows, pl.ds(HALF + offset, LANES)]], axis=1
    )


def put_pair(ref, rows, offset, values):
    ref[rows, pl.ds(offset, LANES)] = values[:, :LANES]
    ref[rows, pl.ds(HALF + offset, LANES)] = values[:, LANES:]


def main_kernel(
    comm,
    lengths,
    tokens_hbm,
    cot_hbm,
    small,
    w_in,
    w_mid,
    w_up,
    w_down,
    *rest,
):
    if not comm:
        whole_hbm, *rest = rest
    (
        out_hbm,
        back,
        shard,
        vectors,
        probs_hbm,
        unit,
        packed,
        context,
        normed,
        inverse,
        first,
        hidden,
        slope,
        own,
        cot,
        flip_a,
        flip_b,
        probs,
        sums,
        up_sums,
        local_sem,
        probs_sem,
        *rest,
    ) = rest
    if comm:
        (sib_in, diag_in, line_in, z_in, send, recv, rs_send, rs_recv) = rest
    micro, per_micro = lengths.shape
    chains = micro * per_micro
    length = own.shape[0] // chains
    count = own.shape[0]

    planes = unit.shape[1]
    if comm:
        rank = lax.axis_index("dp")
        core = lax.axis_index("mp")
        z, y, x = rank // 4, (rank // 2) % 2, rank % 2
        mine = pl.ds(pl.multiple_of(core * HALF, HALF), HALF)
        other = pl.ds(pl.multiple_of((1 - core) * HALF, HALF), HALF)

        def device(zz, yy, xx, cc):
            return (zz * 4 + yy * 2 + xx, cc)

        y1, x1 = jnp.where(core == 0, y, 1 - y), jnp.where(core == 0, 1 - x, x)
        y2, x2 = jnp.where(core == 0, 1 - y, y), jnp.where(core == 0, x, 1 - x)
        near = device(z, y1, x1, core)
        next_ = device(z, y2, x2, core)
        sibling = device(z, y, x, 1 - core)

        def plane(step):
            return lax.rem(z + step, planes)

        def plane_back(step):
            return lax.rem(z + planes - step, planes)

        def remote(src, dst, ssem, rsem, target):
            return pltpu.make_async_remote_copy(
                src_ref=src,
                dst_ref=dst,
                send_sem=ssem,
                recv_sem=rsem,
                device_id=target,
                device_id_type=MESH,
            )

        LINE = planes - 1

        def gz(u, step):
            piece = unit.at[u, z, y, x, :, mine]
            return remote(
                piece, piece, send.at[u, step - 1], recv.at[u, step - 1], device(plane(step), y, x, core)
            )

        def gline(u, which):
            piece = unit.at[u, :, y, x, :, mine]
            return remote(
                piece,
                piece,
                send.at[u, LINE + which],
                recv.at[u, LINE + which],
                near if which else next_,
            )

        def gdiag(u):
            piece = unit.at[u, :, y2, x2, :, mine]
            return remote(piece, piece, send.at[u, LINE + 2], recv.at[u, LINE + 2], near)

        def gsib(u):
            piece = unit.at[u, :, :, :, :, mine]
            return remote(piece, piece, send.at[u, LINE + 3], recv.at[u, LINE + 3], sibling)

        def ag_z(u):
            for step in range(1, planes):
                gz(u, step).start()

        def ag_line(u):
            for step in range(1, planes):
                gz(u, step).wait_recv()
            gline(u, 0).start()
            gline(u, 1).start()

        def ag_diag(u):
            gline(u, 0).wait_recv()
            gdiag(u).start()

        def ag_sib(u):
            gline(u, 1).wait_recv()
            gdiag(u).wait_recv()
            gsib(u).start()

        def ag_ready(u):
            gsib(u).wait_recv()

        def ag_sent(u):
            for step in range(1, planes):
                gz(u, step).wait_send()
            gline(u, 0).wait_send()
            gline(u, 1).wait_send()
            gdiag(u).wait_send()
            gsib(u).wait_send()

        def rsib(u):
            return remote(
                unit.at[u, :, :, :, :, other], sib_in.at[u], rs_send.at[u, 0], rs_recv.at[u, 0], sibling
            )

        def rdiag(u):
            return remote(
                unit.at[u, :, 1 - y, 1 - x, :, mine],
                diag_in.at[u],
                rs_send.at[u, 1],
                rs_recv.at[u, 1],
                near,
            )

        def rline(u, which):
            yy, xx = (y2, x2) if which else (y1, x1)
            return remote(
                unit.at[u, :, yy, xx, :, mine],
                line_in.at[u, which],
                rs_send.at[u, 2 + which],
                rs_recv.at[u, 2 + which],
                next_ if which else near,
            )

        def rz(u, step):
            return remote(
                unit.at[u, plane(step), y, x, :, mine],
                z_in.at[u, step - 1],
                rs_send.at[u, 3 + step],
                rs_recv.at[u, 3 + step],
                device(plane(step), y, x, core),
            )

        def rs_start(u):
            rsib(u).start()

        def rs_own(u):
            rsib(u).wait_recv()

            def add(zz):
                for yy in range(2):
                    for xx in range(2):
                        unit[u, zz, yy, xx, :, mine] = (
                            unit[u, zz, yy, xx, :, mine].astype(f32) + sib_in[u, zz, yy, xx].astype(f32)
                        ).astype(bf16)

            loop(planes, add)
            rdiag(u).start()
            rline(u, 0).start()

        def rs_diag(u):
            rdiag(u).wait_recv()

            def add(zz):
                unit[u, zz, y2, x2, :, mine] = (
                    unit[u, zz, y2, x2, :, mine].astype(f32) + diag_in[u, zz].astype(f32)
                ).astype(bf16)

            loop(planes, add)
            rline(u, 1).start()

        def rs_line(u):
            rline(u, 0).wait_recv()
            rline(u, 1).wait_recv()

            def add(zz):
                unit[u, zz, y, x, :, mine] = (
                    unit[u, zz, y, x, :, mine].astype(f32)
                    + line_in[u, 0, zz].astype(f32)
                    + line_in[u, 1, zz].astype(f32)
                ).astype(bf16)

            loop(planes, add)
            for step in range(1, planes):
                rz(u, step).start()

        def rs_done(u):
            total = unit[u, z, y, x, :, mine].astype(f32)
            for step in range(1, planes):
                rz(u, step).wait_recv()
                total = total + z_in[u, step - 1].astype(f32)
            shard[u] = total

        def rs_sent(u):
            rsib(u).wait_send()
            rdiag(u).wait_send()
            rline(u, 0).wait_send()
            rline(u, 1).wait_send()
            for step in range(1, planes):
                rz(u, step).wait_send()

    def pump(t):
        if not comm:
            return
        if 0 <= t + 3 < UNITS:
            ag_z(t + 3)
        if 0 <= t + 2 < UNITS:
            ag_line(t + 2)
        if 0 <= t + 1 < UNITS:
            ag_diag(t + 1)
        if 0 <= t < UNITS:
            ag_sib(t)

    def ready(u):
        if comm:
            ag_ready(u)

    def weights(u):
        return unit[u].reshape(WIDE, WIDE)

    def unit_cols(u, columns):
        return unit[u, :, :, :, :, columns].reshape(WIDE, columns.size)

    own_copy = pltpu.make_async_copy(tokens_hbm, own, local_sem.at[0])
    cot_copy = pltpu.make_async_copy(cot_hbm, cot, local_sem.at[1])
    out_copy = pltpu.make_async_copy(cot, out_hbm, local_sem.at[2])
    own_copy.start()
    cot_copy.start()

    if comm:
        barrier = pltpu.get_barrier_semaphore()
        greeted = [device(plane(step), y, x, core) for step in range(1, planes)]
        greeted += [near, next_, sibling]
        for target in greeted:
            pl.semaphore_signal(barrier, inc=1, device_id=target, device_id_type=MESH)
        for g in range(3):
            for kind in range(3):
                columns = pl.ds(pl.multiple_of(core * HALF + kind * LANES, LANES), LANES)
                unit[g, z, y, x, :, columns] = w_in[:, kind, pl.ds(g * LANES, LANES)].astype(bf16)
        unit[3, z, y, x, :, mine] = w_mid[...].T.astype(bf16)
        for u in range(4):
            unit[4 + u, z, y, x, :, mine] = w_up[:, pl.ds(u * HALF, HALF)].astype(bf16)
            unit[8 + u, z, y, x, :, mine] = w_down[pl.ds(u * HALF, HALF), :].T.astype(bf16)
        pl.semaphore_wait(barrier, len(greeted))
    else:
        unit_copy = pltpu.make_async_copy(whole_hbm, unit, local_sem.at[3])
        unit_copy.start()
        unit_copy.wait()

    pump(-3)
    sums[...] = jnp.zeros_like(sums)
    up_sums[...] = jnp.zeros_like(up_sums)
    pump(-2)
    own_copy.wait()
    pump(-1)
    pump(0)

    def probs_out(t):
        return pltpu.make_async_copy(probs.at[t % 2], probs_hbm.at[t], probs_sem.at[t % 2])

    def probs_back(t):
        return pltpu.make_async_copy(probs_hbm.at[t], probs.at[t % 2], probs_sem.at[t % 2])

    position = lax.broadcasted_iota(jnp.int32, (1, length), 1)

    for g in range(3):
        ready(g)
        bias = jnp.concatenate(
            [
                piece
                for c in range(2)
                for piece in (
                    small[pl.ds(0, 1), pl.ds(c * HALF + g * LANES, LANES)],
                    jnp.zeros((1, LANES), f32),
                    small[pl.ds(1, 1), pl.ds(c * HALF + g * LANES, LANES)],
                )
            ],
            axis=1,
        )
        lane = lax.broadcasted_iota(jnp.int32, (1, WIDE), 1) % HALF
        scale = jnp.where(lane < LANES, HEAD ** (-0.5), 1.0)

        def project(r):
            rows = tile(r, ROWS)
            for j in range(3):
                cols = pl.ds(j * QUAD, QUAD)
                part = slice(j * QUAD, (j + 1) * QUAD)
                packed[g, rows, cols] = (
                    (nn(own[rows, :], unit_cols(g, cols)) + bias[:, part]).astype(bf16).astype(f32)
                    * scale[:, part]
                ).astype(bf16)

        loop(count // ROWS, project)
        pump(1 + 2 * g)

        def attend(chain):
            t = g * chains + chain

            @pl.when(t >= 2)
            def _():
                probs_out(t - 2).wait()

            rows = tile(chain, length)
            here = packed.at[g]
            queries = spread_heads(pair(here, rows, 0))
            keys = pair(here, rows, LANES)
            values = pair(here, rows, 2 * LANES)
            limit = lengths[chain // per_micro, chain % per_micro]
            scores = jnp.where(position < limit, nt(queries, keys), MASKED_SCORE)
            peak = jnp.max(scores, axis=1, keepdims=True)
            exponent = jnp.exp(scores - peak)
            total = jnp.sum(exponent, axis=1, keepdims=True)
            low = (exponent * (1.0 / total)).astype(bf16)
            probs[t % 2] = low
            probs_out(t).start()
            mixed = pick_heads(nn(low, values), length).astype(bf16)
            put_pair(context, rows, g * LANES, mixed)

        def attend_first(chain):
            attend(chain)

        def attend_second(chain):
            attend(chain + chains // 2)

        loop(chains // 2, attend_first)
        pump(2 + 2 * g)
        loop(chains - chains // 2, attend_second)

    ready(3)

    def mid(r):
        rows = tile(r, ROWS)
        back[rows, :] = nt(context[rows, :], weights(3))

    loop(count // ROWS, mid)

    def first_norm(r):
        rows = tile(r, BLOCK)
        value = own[rows, :].astype(f32) + back[rows, :] + small[pl.ds(2, 1), :]
        center = value - mean_last(value)
        root = lax.rsqrt(mean_last(center * center) + NORM_EPS)
        scaled = center * root
        normed[rows, :] = scaled
        inverse[rows, :] = root
        first[rows, :] = (scaled * small[pl.ds(3, 1), :] + small[pl.ds(4, 1), :]).astype(bf16)

    loop(count // BLOCK, first_norm)
    pump(7)

    def up(u):
        ready(4 + u)
        bias = jnp.concatenate(
            [
                small[pl.ds(8 + c * 2 + u // 2, 1), pl.ds((u % 2) * HALF, HALF)]
                for c in range(2)
            ],
            axis=1,
        )

        def block(r):
            rows = tile(r, ROWS)
            for j in range(3):
                cols = pl.ds(j * QUAD, QUAD)
                upper = nn(first[rows, :], unit_cols(4 + u, cols)) + bias[:, j * QUAD : (j + 1) * QUAD]
                share = 0.5 + 0.5 * lax.erf(upper * 0.7071067811865476)
                hidden[u, rows, cols] = (upper * share).astype(bf16)
                slope[u, rows, cols] = (
                    share + upper * (0.3989422804014327 * jnp.exp(-0.5 * upper * upper))
                ).astype(bf16)

        loop(count // ROWS, block)

    def down(u):
        ready(8 + u)

        def block(r):
            rows = tile(r, ROWS)
            term = nt(hidden[u, rows, :], weights(8 + u))
            back[rows, :] = term if u == 0 else back[rows, :] + term

        loop(count // ROWS, block)

    up(0)
    up(1)
    pump(8)
    up(2)
    pump(9)
    up(3)
    down(0)
    pump(10)
    down(1)
    pump(11)
    down(2)
    down(3)
    if comm:
        for u in range(UNITS):
            ag_sent(u)
    cot_copy.wait()

    def flip(source, target):
        for j in range(WIDE // LANES):
            cols = pl.ds(j * LANES, LANES)
            target[cols, :] = source[:, cols].T

    def second_norm(r):
        rows = tile(r, BLOCK)
        value = (
            normed[rows, :] * small[pl.ds(3, 1), :]
            + small[pl.ds(4, 1), :]
            + back[rows, :]
            + small[pl.ds(5, 1), :]
        )
        center = value - mean_last(value)
        root = lax.rsqrt(mean_last(center * center) + NORM_EPS)
        scaled = center * root
        upstream = cot[rows, :].astype(f32)
        cot[rows, :] = (scaled * small[pl.ds(6, 1), :] + small[pl.ds(7, 1), :]).astype(bf16)
        gained = upstream * small[pl.ds(6, 1), :]
        grad = (gained - mean_last(gained) - scaled * mean_last(gained * scaled)) * root
        back[rows, :] = grad
        low = grad.astype(bf16)
        own[rows, :] = low
        sums[5] += fold_rows(low.astype(f32))
        sums[6] += fold_rows(upstream * scaled)
        sums[7] += fold_rows(upstream)

    loop(count // BLOCK, second_norm)
    out_copy.start()
    flip(own, flip_a)
    flip(first, flip_b)

    def outer(u, flipped, source):
        def block(r):
            part = nn(flipped[tile(r, WIDE // planes), :], source[...]).astype(bf16)
            unit[u, r] = part.reshape(unit.shape[2:])

        loop(planes, block)

    for u in range(4):

        def block(r, u=u):
            rows = tile(r, ROWS)
            for j in range(3):
                cols = pl.ds(j * QUAD, QUAD)
                low = (nn(own[rows, :], unit_cols(8 + u, cols)) * slope[u, rows, cols].astype(f32)).astype(
                    bf16
                )
                slope[u, rows, cols] = low
                up_sums[u, :, cols] += fold_rows(low.astype(f32))

        loop(count // ROWS, block)
        outer(8 + u, flip_a, hidden.at[u])
        if comm:
            rs_start(8 + u)

        def gather_first(r, u=u):
            rows = tile(r, ROWS)
            back[rows, :] += nt(slope[u, rows, :], weights(4 + u))

        loop(count // ROWS, gather_first)
        outer(4 + u, flip_b, slope.at[u])
        if comm:
            rs_start(4 + u)
            rs_own(8 + u)
            if u >= 1:
                rs_own(4 + u - 1)
                rs_diag(8 + u - 1)
            if u >= 2:
                rs_diag(4 + u - 2)
                rs_line(8 + u - 2)

    def first_back(r):
        rows = tile(r, BLOCK)
        upstream = back[rows, :]
        scaled = normed[rows, :]
        gained = upstream * small[pl.ds(3, 1), :]
        grad = (gained - mean_last(gained) - scaled * mean_last(gained * scaled)) * inverse[rows, :]
        back[rows, :] = grad
        low = grad.astype(bf16)
        own[rows, :] = low
        sums[2] += fold_rows(low.astype(f32))
        sums[3] += fold_rows(upstream * scaled)
        sums[4] += fold_rows(upstream)

    loop(count // BLOCK, first_back)
    if comm:
        rs_own(7)
        rs_diag(11)
        rs_diag(6)
        rs_line(10)
        rs_line(4)
        rs_done(8)
    out_copy.wait()
    flip(own, flip_a)

    def mid_back(r):
        rows = tile(r, ROWS)
        for j in range(3):
            cols = pl.ds(j * QUAD, QUAD)
            cot[rows, cols] = nn(own[rows, :], unit_cols(3, cols)).astype(bf16)

    loop(count // ROWS, mid_back)
    for t in (chains * 3 - 2, chains * 3 - 1):
        probs_out(t).wait()
    probs_back(0).start()
    outer(3, flip_a, context)
    if comm:
        rs_start(3)
    own_again = pltpu.make_async_copy(tokens_hbm, own, local_sem.at[0])
    own_again.start()
    if comm:
        rs_diag(7)
        rs_line(11)
        rs_line(5)
        rs_done(9)
    own_again.wait()
    flip(own, flip_b)
    if comm:
        rs_own(3)

    for g in range(3):
        grads = hidden.at[g]

        def attend_back(chain):
            t = g * chains + chain
            probs_back(t).wait()

            @pl.when(t + 1 < 3 * chains)
            def _():
                probs_back(t + 1).start()

            rows = tile(chain, length)
            here = packed.at[g]
            queries = spread_heads(pair(here, rows, 0))
            keys = pair(here, rows, LANES)
            values = pair(here, rows, 2 * LANES)
            d_context = spread_heads(pair(cot, rows, g * LANES))
            low = probs[t % 2]
            wide = low.astype(f32)
            d_probs = nt(d_context, values)
            inner = jnp.sum(wide * d_probs, axis=1, keepdims=True)
            d_scores = (wide * (d_probs - inner)).astype(bf16)
            d_queries = (pick_heads(nn(d_scores, keys), length) * HEAD ** (-0.5)).astype(bf16)
            d_keys = tn(d_scores, queries).astype(bf16)
            d_values = tn(low, d_context).astype(bf16)
            put_pair(grads, rows, 0, d_queries)
            put_pair(grads, rows, LANES, d_keys)
            put_pair(grads, rows, 2 * LANES, d_values)
            for row, piece in ((0, d_queries), (1, d_values)):
                folded = fold_rows(piece.astype(f32))
                for c in range(2):
                    cols = pl.ds(c * HALF + g * LANES, LANES)
                    sums[row, :, cols] += folded[:, c * LANES : (c + 1) * LANES]

        def back_first(chain):
            attend_back(chain)

        def back_second(chain):
            attend_back(chain + chains // 2)

        loop(chains // 2, back_first)
        if comm:
            if g == 0:
                rs_line(6)
                rs_done(10)
                rs_done(4)
            if g == 1:
                rs_own(0)
                rs_diag(3)
                rs_done(11)
                rs_done(5)
            if g == 2:
                rs_own(1)
                rs_diag(0)
                rs_line(3)
                rs_done(7)
        loop(chains - chains // 2, back_second)

        def tokens_back(r):
            rows = tile(r, ROWS)
            back[rows, :] += nt(grads[rows, :], weights(g))

        loop(count // ROWS, tokens_back)
        outer(g, flip_b, grads)
        if comm:
            rs_start(g)
            if g == 0:
                rs_line(7)
                rs_done(6)

    if comm:
        rs_own(2)
        rs_diag(1)
        rs_line(0)
        rs_done(3)
        rs_diag(2)
        rs_line(1)
        rs_done(0)
        rs_line(2)
        rs_done(1)
        rs_done(2)
        for u in range(UNITS):
            rs_sent(u)
    else:
        whole_out = pltpu.make_async_copy(unit, shard, local_sem.at[3])
        whole_out.start()
        whole_out.wait()

    vectors[pl.ds(0, 8), :] = jnp.sum(sums[...], axis=1)
    folded = jnp.sum(up_sums[...], axis=1)
    for u in range(4):
        for c in range(2):
            vectors[pl.ds(8 + c * 2 + u // 2, 1), pl.ds((u % 2) * HALF, HALF)] = folded[
                u : u + 1, c * HALF : (c + 1) * HALF
            ]


def run_layer(tokens, lengths, cotangent, attn_in, attn_out, ffn_in, ffn_out, small, ranks):
    rows_here = attn_in.shape[0]
    width = small.shape[1]
    flat = tokens.reshape(-1, width)
    count = flat.shape[0]
    chains = lengths.size
    length = tokens.shape[2]
    comm = ranks % 4 == 0 and rows_here % 16 == 0
    planes = ranks // 4 if comm else 4
    steps = planes - 1
    unit_shape = (UNITS, planes, 2, 2, width // (planes * 4), WIDE)
    vmem = pl.BlockSpec(memory_space=pltpu.VMEM)
    hbm = pl.BlockSpec(memory_space=pl.ANY)
    operands = [lengths, flat, cotangent.reshape(-1, width), small, attn_in, attn_out, ffn_in, ffn_out]
    in_specs = [pl.BlockSpec(memory_space=pltpu.SMEM), hbm, hbm] + [vmem] * 5
    if not comm:
        shard = own_shard(attn_in, attn_out, ffn_in, ffn_out)
        whole = lax.all_gather(shard, "dp", axis=1, tiled=True)
        whole = lax.all_gather(whole, "mp", axis=2, tiled=True)
        operands.append(whole.reshape(unit_shape))
        in_specs.append(hbm)
    shard_shape = (UNITS, rows_here, HALF)
    out_shape = (
        jax.ShapeDtypeStruct((count, width), bf16),
        jax.ShapeDtypeStruct((count, width), f32),
        jax.ShapeDtypeStruct(shard_shape, f32) if comm else jax.ShapeDtypeStruct(unit_shape, bf16),
        jax.ShapeDtypeStruct(small.shape, f32),
        jax.ShapeDtypeStruct((3 * chains, 4 * length, length), bf16),
    )
    out_specs = (hbm, vmem, vmem if comm else hbm, vmem, hbm)
    scratch = [
        pltpu.VMEM(unit_shape, bf16),
        pltpu.VMEM((3, count, WIDE), bf16),
        pltpu.VMEM((count, width), bf16),
        pltpu.VMEM((count, width), f32),
        pltpu.VMEM((count, 1), f32),
        pltpu.VMEM((count, width), bf16),
        pltpu.VMEM((4, count, WIDE), bf16),
        pltpu.VMEM((4, count, WIDE), bf16),
        pltpu.VMEM((count, width), bf16),
        pltpu.VMEM((count, width), bf16),
        pltpu.VMEM((width, count), bf16),
        pltpu.VMEM((width, count), bf16),
        pltpu.VMEM((2, 4 * length, length), bf16),
        pltpu.VMEM((8, 8, width), f32),
        pltpu.VMEM((4, 8, WIDE), f32),
        pltpu.SemaphoreType.DMA((4,)),
        pltpu.SemaphoreType.DMA((2,)),
    ]
    params = dict(vmem_limit_bytes=64 * 2**20 - 2**16)
    if comm:
        scratch += [
            pltpu.VMEM((UNITS, planes, 2, 2, rows_here, HALF), bf16),
            pltpu.VMEM((UNITS, planes, rows_here, HALF), bf16),
            pltpu.VMEM((UNITS, 2, planes, rows_here, HALF), bf16),
            pltpu.VMEM((UNITS, steps, rows_here, HALF), bf16),
            pltpu.SemaphoreType.DMA((UNITS, steps + 4)),
            pltpu.SemaphoreType.DMA((UNITS, steps + 4)),
            pltpu.SemaphoreType.DMA((UNITS, steps + 4)),
            pltpu.SemaphoreType.DMA((UNITS, steps + 4)),
        ]
        params.update(collective_id=0, has_side_effects=True)
    out, back, shard, vectors, _ = pl.pallas_call(
        functools.partial(main_kernel, comm),
        out_shape=out_shape,
        in_specs=in_specs,
        out_specs=out_specs,
        scratch_shapes=scratch,
        compiler_params=pltpu.CompilerParams(**params),
    )(*operands)
    if not comm:
        summed = shard.reshape(UNITS, width, 2, HALF).astype(f32)
        summed = lax.psum_scatter(summed, "mp", scatter_dimension=2, tiled=True)
        summed = lax.psum_scatter(
            summed.reshape(UNITS, width, HALF), "dp", scatter_dimension=1, tiled=True
        )
        shard = summed
    return out.reshape(tokens.shape), back.reshape(tokens.shape), shard, vectors


def own_shard(attn_in, attn_out, ffn_in, ffn_out):
    rows = attn_in.shape[0]
    heads = [
        attn_in[:, :, g * LANES : (g + 1) * LANES].reshape(rows, HALF) for g in range(3)
    ]
    up = [ffn_in[:, u * HALF : (u + 1) * HALF] for u in range(4)]
    down = [ffn_out[u * HALF : (u + 1) * HALF].T for u in range(4)]
    return jnp.stack(heads + [attn_out.T] + up + down).astype(bf16)


def adam_moments(gradient, first_moment, second_moment):
    first_new = BETA_FIRST * first_moment + (1.0 - BETA_FIRST) * gradient
    second_new = BETA_SECOND * second_moment + (1.0 - BETA_SECOND) * gradient * gradient
    direction = (
        first_new
        / (1.0 - BETA_FIRST**STEP)
        / (jnp.sqrt(second_new / (1.0 - BETA_SECOND**STEP)) + ADAM_EPS)
    )
    return (first_new, second_new, direction)


def body(
    ranks,
    tokens,
    lengths,
    cotangent,
    attn_in,
    attn_out,
    ffn_in,
    ffn_out,
    attn_in_first,
    attn_in_second,
    attn_out_first,
    attn_out_second,
    ffn_in_first,
    ffn_in_second,
    ffn_out_first,
    ffn_out_second,
    small,
    small_first,
    small_second,
):
    output, tokens_grad, shard, vectors = run_layer(
        tokens, lengths, cotangent, attn_in, attn_out, ffn_in, ffn_out, small, ranks
    )
    rows = attn_in.shape[0]
    grad_in = jnp.concatenate([shard[g].reshape(rows, 3, LANES) for g in range(3)], axis=2)
    grad_mid = shard[3].T
    grad_up = jnp.concatenate([shard[4 + u] for u in range(4)], axis=1)
    grad_down = jnp.concatenate([shard[8 + u].T for u in range(4)], axis=0)
    matrices = (
        (attn_in, grad_in, attn_in_first, attn_in_second),
        (attn_out, grad_mid, attn_out_first, attn_out_second),
        (ffn_in, grad_up, ffn_in_first, ffn_in_second),
        (ffn_out, grad_down, ffn_out_first, ffn_out_second),
    )
    moments = [adam_moments(entry[1], entry[2], entry[3]) for entry in matrices]
    headings = [moments[i][2] + DECAY_RATE * matrices[i][0] for i in range(4)]
    weight_squares = jnp.stack([jnp.sum(entry[0] * entry[0]) for entry in matrices])
    step_squares = jnp.stack([jnp.sum(heading * heading) for heading in headings])
    vector_grad, weight_sums, step_sums = lax.psum(
        (vectors, weight_squares, step_squares), ("dp", "mp")
    )
    weight_norms = jnp.sqrt(weight_sums)
    step_norms = jnp.sqrt(step_sums)
    results = [output, tokens_grad]
    for i in range(4):
        weight = matrices[i][0]
        renewed = weight - RATE_MATRIX * (weight_norms[i] / step_norms[i]) * headings[i]
        results.extend(
            [matrices[i][1], moments[i][0], moments[i][1], renewed, renewed.astype(bf16)]
        )
    small_first_new, small_second_new, small_direction = adam_moments(
        vector_grad, small_first, small_second
    )
    small_new = small - RATE_VECTOR * small_direction
    results.extend(
        [
            vector_grad,
            small_first_new,
            small_second_new,
            small_new,
            jnp.stack((weight_norms, step_norms)),
        ]
    )
    return tuple(results)


def solution(mesh):
    chains = P(None, ("dp", "mp"), None, None)
    rows_three = P("dp", None, "mp")
    rows_two = P("dp", "mp")
    columns = P("mp", "dp")
    whole = P()
    return jax.shard_map(
        functools.partial(body, mesh.shape["dp"]),
        mesh=mesh,
        in_specs=(
            chains,
            P(None, ("dp", "mp")),
            chains,
            rows_three,
            columns,
            rows_two,
            columns,
            rows_three,
            rows_three,
            columns,
            columns,
            rows_two,
            rows_two,
            columns,
            columns,
            whole,
            whole,
            whole,
        ),
        out_specs=(
            (chains, chains)
            + (rows_three,) * 5
            + (columns,) * 5
            + (rows_two,) * 5
            + (columns,) * 5
            + (whole,) * 5
        ),
        check_vma=False,
    )
```

```python
import functools

import jax
import jax.numpy as jnp
from jax import lax
from jax.experimental import pallas as pl
from jax.experimental.pallas import tpu as pltpu
from jax.sharding import PartitionSpec as P

HEAD = 64
STEP = 10
NORM_EPS = 1e-05
RATE_MATRIX = 0.3
RATE_VECTOR = 0.2
BETA_FIRST = 0.9
BETA_SECOND = 0.999
ADAM_EPS = 1e-06
DECAY_RATE = 0.01
MASKED_SCORE = -1000000000.0

MESH = pl.DeviceIdType.MESH
bf16, f32 = jnp.bfloat16, jnp.float32
UNITS = 12
HALF = 384
MATRIX_OF = (0, 0, 0, 1, 2, 2, 2, 2, 3, 3, 3, 3)
WIDE = 768
LANES = 128
QUAD = 256
BLOCK = 192
G_SLOT = {2: 9, 1: 10, 0: 8}
PLANES, LINES, DIAGONAL, SIBLING, OWN, DONE, SHARDS = range(7)
SPLIT_GATHER = (5, 7, 9, 10)
SPLIT_SUMS = (8, 4, 9, 5)
GATHER = (
    ((PLANES, 0), (PLANES, 1), (PLANES, 2),),
    ((LINES, 0), (PLANES, 3), (LINES, 1), (PLANES, 4), (DIAGONAL, 0), (PLANES, 5), (LINES, 2), (PLANES, 6), (DIAGONAL, 1), (PLANES, 7), (LINES, 3), (PLANES, 8), (SIBLING, 0), (PLANES, 9), (SHARDS, 5), (PLANES, 10),),
    (),
    ((DIAGONAL, 2), (PLANES, 11), (LINES, 4),),
    ((SHARDS, 7), (SIBLING, 1), (LINES, 5),),
    (),
    ((DIAGONAL, 3),),
    ((SHARDS, 9), (SHARDS, 10), (LINES, 6),),
    ((SIBLING, 2), (LINES, 7),),
    (),
    ((DIAGONAL, 4),),
    ((LINES, 8),),
    ((SIBLING, 3), (LINES, 9),),
    (),
    ((DIAGONAL, 6),),
    ((DIAGONAL, 5),),
    ((SIBLING, 4), (LINES, 10),),
    (),
    ((DIAGONAL, 8), (LINES, 11), (SIBLING, 6), (DIAGONAL, 7), (SIBLING, 5),),
    (),
    (),
    ((SIBLING, 8), (DIAGONAL, 9),),
    ((DIAGONAL, 10), (DIAGONAL, 11), (SIBLING, 7),),
    ((SIBLING, 9),),
    (),
    ((SIBLING, 10),),
    (),
    ((SIBLING, 11),),
    (),
    (),
    (),
    (),
)
REDUCE = (
    (),
    (),
    (),
    ((OWN, 8),),
    ((OWN, 4),),
    (),
    ((DIAGONAL, 8), (OWN, 9), (LINES, 8),),
    ((DIAGONAL, 4),),
    ((LINES, 4), (OWN, 5),),
    ((SHARDS, 8), (DIAGONAL, 9),),
    ((LINES, 9), (OWN, 10),),
    ((DIAGONAL, 5),),
    ((LINES, 5), (OWN, 6),),
    ((SHARDS, 4), (DIAGONAL, 10),),
    ((OWN, 11),),
    ((DIAGONAL, 6),),
    ((OWN, 7), (SHARDS, 9),),
    ((LINES, 10), (DONE, 8), (DONE, 4),),
    ((DIAGONAL, 11),),
    (),
    (),
    ((SHARDS, 5), (DIAGONAL, 7), (LINES, 6), (OWN, 3),),
    ((DONE, 9),),
    ((LINES, 11), (DONE, 5),),
    ((LINES, 7), (OWN, 2), (DONE, 10), (DIAGONAL, 3),),
    ((DONE, 6),),
    ((DIAGONAL, 2),),
    ((OWN, 1), (DONE, 11), (LINES, 3),),
    ((LINES, 2), (DONE, 7),),
    ((DIAGONAL, 1),),
    ((OWN, 0), (DONE, 3),),
    ((LINES, 1),),
    ((DIAGONAL, 0), (DONE, 2),),
    ((DONE, 1), (LINES, 0), (DONE, 0),),
)


def nn(left, right):
    return lax.dot_general(left, right, (((1,), (0,)), ((), ())), preferred_element_type=f32)


def nt(left, right):
    return lax.dot_general(left, right, (((1,), (1,)), ((), ())), preferred_element_type=f32)


def tn(left, right):
    return lax.dot_general(left, right, (((0,), (0,)), ((), ())), preferred_element_type=f32)


def tile(index, size):
    if isinstance(index, int):
        return pl.ds(index * size, size)
    return pl.ds(pl.multiple_of(index * size, size), size)


def loop(count, body):
    def step(index, carry):
        body(index)
        return carry

    if count == 1:
        body(0)
    else:
        lax.fori_loop(0, count, step, 0)


def mean_last(values):
    return jnp.sum(values, axis=-1, keepdims=True) * (1.0 / values.shape[-1])


def fold_rows(values):
    return jnp.sum(values.reshape(values.shape[0] // 8, 8, values.shape[1]), axis=0)


def fold_tile(values):
    folded = fold_rows(values)
    return sum(folded[:, c : c + LANES] for c in range(0, folded.shape[1], LANES))


def unit_part(refs, u):
    if u < 3:
        return jnp.concatenate([refs[0][k, :, pl.ds(u * LANES, LANES)] for k in range(3)], axis=1)
    if u == 3:
        return refs[1][...]
    return refs[2 + (u - 4) // 4][:, pl.ds((u % 4) * HALF, HALF)]


def adam_moments(gradient, first_moment, second_moment):
    first_new = BETA_FIRST * first_moment + (1.0 - BETA_FIRST) * gradient
    second_new = BETA_SECOND * second_moment + (1.0 - BETA_SECOND) * gradient * gradient
    direction = (
        first_new
        / (1.0 - BETA_FIRST**STEP)
        / (jnp.sqrt(second_new / (1.0 - BETA_SECOND**STEP)) + ADAM_EPS)
    )
    return (first_new, second_new, direction)


def head_lane():
    return lax.broadcasted_iota(jnp.int32, (1, QUAD), 1) // HEAD


def spread_heads(values):
    lane = head_lane()
    zero = jnp.zeros_like(values)
    return jnp.concatenate([jnp.where(lane == head, values, zero) for head in range(4)], axis=0)


def pick_heads(values, length):
    lane = head_lane()
    result = values[:length]
    for head in range(1, 4):
        result = jnp.where(lane == head, values[head * length : (head + 1) * length], result)
    return result


def pair(ref, rows, offset):
    return jnp.concatenate(
        [ref[rows, pl.ds(offset, LANES)], ref[rows, pl.ds(HALF + offset, LANES)]], axis=1
    )


def put_pair(ref, rows, offset, values):
    ref[rows, pl.ds(offset, LANES)] = values[:, :LANES]
    ref[rows, pl.ds(HALF + offset, LANES)] = values[:, LANES:]


def main_kernel(
    comm,
    lengths,
    tokens_hbm,
    cot_hbm,
    small,
    w_in,
    w_mid,
    w_up,
    w_down,
    *rest,
):
    if comm:
        *moments_hbm, out_hbm, back_hbm, shard, vectors, norms, probs_hbm = rest[:14]
        rest = rest[14:]
    else:
        whole_hbm, out_hbm, back_hbm, shard, vectors, probs_hbm = rest[:6]
        rest = rest[6:]
    (
        back,
        unit,
        packed,
        context,
        normed,
        inverse,
        first,
        hidden,
        slope,
        own,
        cot,
        flip_a,
        flip_b,
        probs,
        sums,
        up_sums,
        local_sem,
        probs_sem,
        *rest,
    ) = rest
    if comm:
        sib_in, diag_in, line_in, z_in, *rest = rest
        squares, square_in, vec_sum, vec_in, vec_z_in = rest[:5]
        send, recv, rs_send, rs_recv, vec_send, vec_recv, square_send, square_recv, held_sem, shard_sem = rest[5:]
    micro, per_micro = lengths.shape
    chains = micro * per_micro
    length = own.shape[0] // chains
    count = own.shape[0]

    planes = unit.shape[1]
    if comm:
        rank = lax.axis_index("dp")
        core = lax.axis_index("mp")
        z, y, x = rank // 4, (rank // 2) % 2, rank % 2
        mine = pl.ds(pl.multiple_of(core * HALF, HALF), HALF)
        other = pl.ds(pl.multiple_of((1 - core) * HALF, HALF), HALF)

        def device(zz, yy, xx, cc):
            return (zz * 4 + yy * 2 + xx, cc)

        y1, x1 = jnp.where(core == 0, y, 1 - y), jnp.where(core == 0, 1 - x, x)
        y2, x2 = jnp.where(core == 0, 1 - y, y), jnp.where(core == 0, x, 1 - x)
        near = device(z, y1, x1, core)
        next_ = device(z, y2, x2, core)
        sibling = device(z, y, x, 1 - core)

        def plane(step):
            return lax.rem(z + step, planes)

        def plane_back(step):
            return lax.rem(z + planes - step, planes)

        def remote(src, dst, ssem, rsem, target):
            return pltpu.make_async_remote_copy(
                src_ref=src,
                dst_ref=dst,
                send_sem=ssem,
                recv_sem=rsem,
                device_id=target,
                device_id_type=MESH,
            )

        LINE = planes - 1

        def gz(u, step):
            piece = unit.at[u, z, y, x, :, mine]
            return remote(
                piece, piece, send.at[u, step - 1], recv.at[u, step - 1], device(plane(step), y, x, core)
            )

        def gline(u, which):
            piece = unit.at[u, :, y, x, :, mine]
            return remote(
                piece,
                piece,
                send.at[u, LINE + which],
                recv.at[u, LINE + which],
                near if which else next_,
            )

        def gdiag(u):
            piece = unit.at[u, :, y2, x2, :, mine]
            return remote(piece, piece, send.at[u, LINE + 2], recv.at[u, LINE + 2], near)

        def gsib(u):
            piece = unit.at[u, :, :, :, :, mine]
            return remote(piece, piece, send.at[u, LINE + 3], recv.at[u, LINE + 3], sibling)

        def gshard(u):
            piece = unit.at[u, z, y, x, :, mine]
            return remote(piece, piece, send.at[u, LINE], recv.at[u, LINE], next_)

        def gz_next(u, step):
            piece = unit.at[u, z, y2, x2, :, mine]
            sem = LINE + 3 + step
            return remote(piece, piece, send.at[u, sem], recv.at[u, sem], device(plane(step), y, x, core))

        def ag_z(u):
            for step in range(1, planes):
                gz(u, step).start()
            if u in SPLIT_GATHER:
                gshard(u).start()

        def ag_shard(u):
            gshard(u).wait_recv()
            for step in range(1, planes):
                gz_next(u, step).start()

        def ag_line(u):
            for step in range(1, planes):
                gz(u, step).wait_recv()
            if u not in SPLIT_GATHER:
                gline(u, 0).start()
            gline(u, 1).start()

        def ag_diag(u):
            if u in SPLIT_GATHER:
                for step in range(1, planes):
                    gz_next(u, step).wait_recv()
            else:
                gline(u, 0).wait_recv()
            gdiag(u).start()

        def ag_sib(u):
            gline(u, 1).wait_recv()
            gdiag(u).wait_recv()
            gsib(u).start()

        def ag_ready(u):
            gsib(u).wait_recv()

        def ag_sent(u):
            for step in range(1, planes):
                gz(u, step).wait_send()
            if u in SPLIT_GATHER:
                gshard(u).wait_send()
                for step in range(1, planes):
                    gz_next(u, step).wait_send()
            else:
                gline(u, 0).wait_send()
            gline(u, 1).wait_send()
            gdiag(u).wait_send()
            gsib(u).wait_send()

        def slot(u):
            return G_SLOT.get(u, u)

        def rsib(u):
            return remote(
                unit.at[slot(u), :, :, :, :, other], sib_in.at[u], rs_send.at[u, 0], rs_recv.at[u, 0], sibling
            )

        def rdiag(u):
            return remote(
                unit.at[slot(u), :, 1 - y, 1 - x, :, mine],
                diag_in.at[u],
                rs_send.at[u, 1],
                rs_recv.at[u, 1],
                near,
            )

        def rline(u, which):
            yy, xx = (y2, x2) if which else (y1, x1)
            return remote(
                unit.at[slot(u), :, yy, xx, :, mine],
                line_in.at[u, which],
                rs_send.at[u, 2 + which],
                rs_recv.at[u, 2 + which],
                next_ if which else near,
            )

        def rz(u, step):
            return remote(
                unit.at[slot(u), plane(step), y, x, :, mine],
                z_in.at[u, step - 1],
                rs_send.at[u, 3 + step],
                rs_recv.at[u, 3 + step],
                device(plane(step), y, x, core),
            )

        def rz_next(u, step):
            sem = 3 + planes + step - 1
            return remote(
                unit.at[slot(u), plane(step), y2, x2, :, mine],
                line_in.at[u, 1, step - 1],
                rs_send.at[u, sem],
                rs_recv.at[u, sem],
                device(plane(step), y, x, core),
            )

        def rshard(u):
            return remote(
                unit.at[slot(u), z, y2, x2, :, mine],
                line_in.at[u, 1, planes - 1],
                rs_send.at[u, 3],
                rs_recv.at[u, 3],
                next_,
            )

        def rs_start(u):
            rsib(u).start()

        def rs_own(u):
            rsib(u).wait_recv()

            def add(zz):
                for yy in range(2):
                    for xx in range(2):
                        unit[slot(u), zz, yy, xx, :, mine] = (
                            unit[slot(u), zz, yy, xx, :, mine].astype(f32) + sib_in[u, zz, yy, xx].astype(f32)
                        ).astype(bf16)

            loop(planes, add)
            rdiag(u).start()
            rline(u, 0).start()

        def rs_diag(u):
            rdiag(u).wait_recv()

            def add(zz):
                unit[slot(u), zz, y2, x2, :, mine] = (
                    unit[slot(u), zz, y2, x2, :, mine].astype(f32) + diag_in[u, zz].astype(f32)
                ).astype(bf16)

            loop(planes, add)
            if u in SPLIT_SUMS:
                for step in range(1, planes):
                    rz_next(u, step).start()
            else:
                rline(u, 1).start()

        def rs_shard(u):
            total = unit[slot(u), z, y2, x2, :, mine].astype(f32)
            for step in range(1, planes):
                rz_next(u, step).wait_recv()
                total = total + line_in[u, 1, step - 1].astype(f32)
            unit[slot(u), z, y2, x2, :, mine] = total.astype(bf16)
            rshard(u).start()

        def rs_line(u):
            rline(u, 0).wait_recv()
            if u not in SPLIT_SUMS:
                rline(u, 1).wait_recv()

            def add(zz):
                total = unit[slot(u), zz, y, x, :, mine].astype(f32) + line_in[u, 0, zz].astype(f32)
                if u not in SPLIT_SUMS:
                    total = total + line_in[u, 1, zz].astype(f32)
                unit[slot(u), zz, y, x, :, mine] = total.astype(bf16)

            loop(planes, add)
            for step in range(1, planes):
                rz(u, step).start()

        def rs_done(u):
            total = unit[slot(u), z, y, x, :, mine].astype(f32)
            for step in range(1, planes):
                rz(u, step).wait_recv()
                total = total + z_in[u, step - 1].astype(f32)
            if u in SPLIT_SUMS:
                rshard(u).wait_recv()
                total = total + line_in[u, 1, planes - 1].astype(f32)
            _, _, direction = adam_moments(total, normed[held(0, u)], normed[held(1, u)])
            weight = normed[held(2, u)]
            normed[held(0, u)] = total
            shard_copy(u).start()
            heading = direction + DECAY_RATE * weight
            which = MATRIX_OF[u]
            squares[which] += fold_tile(weight * weight)
            squares[4 + which] += fold_tile(heading * heading)

        def held(which, u):
            rows = normed.shape[0] // 20
            row = (which * UNITS + u) // 2 * rows
            return pl.ds(row, rows), pl.ds((u % 2) * HALF, HALF)

        def held_copies(which):
            matrices = (moments_hbm[:4], moments_hbm[4:], (w_in, w_mid, w_up, w_down))[which]
            copies = []
            for u in range(UNITS):
                rows, cols = held(which, u)
                if u < 3:
                    pairs = [
                        (
                            matrices[0].at[k, :, pl.ds(u * LANES, LANES)],
                            normed.at[rows, pl.ds(cols.start + k * LANES, LANES)],
                        )
                        for k in range(3)
                    ]
                elif u == 3:
                    pairs = [(matrices[1], normed.at[rows, cols])]
                else:
                    piece = matrices[2 + (u - 4) // 4].at[:, pl.ds((u % 4) * HALF, HALF)]
                    pairs = [(piece, normed.at[rows, cols])]
                for source, target in pairs:
                    sem = held_sem.at[which, len(copies)]
                    copies.append(pltpu.make_async_copy(source, target, sem))
            return copies

        def shard_copy(u):
            return pltpu.make_async_copy(normed.at[held(0, u)], shard.at[u], shard_sem.at[u])

        def rs_sent(u):
            rsib(u).wait_send()
            rdiag(u).wait_send()
            rline(u, 0).wait_send()
            if u in SPLIT_SUMS:
                rshard(u).wait_send()
                for step in range(1, planes):
                    rz_next(u, step).wait_send()
            else:
                rline(u, 1).wait_send()
            for step in range(1, planes):
                rz(u, step).wait_send()

    if comm:
        gathers = {
            PLANES: ag_z,
            SHARDS: ag_shard,
            LINES: ag_line,
            DIAGONAL: ag_diag,
            SIBLING: ag_sib,
        }
        sums_of = {
            OWN: rs_own,
            DIAGONAL: rs_diag,
            SHARDS: rs_shard,
            LINES: rs_line,
            DONE: rs_done,
        }
    gather_plan, reduce_plan = iter(GATHER), iter(REDUCE)

    def gather():
        for kind, u in next(gather_plan):
            if comm:
                gathers[kind](u)

    def reduce():
        for kind, u in next(reduce_plan):
            if comm:
                sums_of[kind](u)

    def ready(u):
        if comm:
            ag_ready(u)

    def weights(u):
        return unit[u].reshape(WIDE, WIDE)

    def unit_cols(u, columns):
        return unit[u, :, :, :, :, columns].reshape(WIDE, columns.size)

    own_copy = pltpu.make_async_copy(tokens_hbm, own, local_sem.at[0])
    cot_copy = pltpu.make_async_copy(cot_hbm, cot, local_sem.at[1])
    out_copy = pltpu.make_async_copy(cot, out_hbm, local_sem.at[2])
    back_copy = pltpu.make_async_copy(back, back_hbm, local_sem.at[3])
    if comm:
        weight_copies = held_copies(2)
        for copy in weight_copies:
            copy.start()
    own_copy.start()
    cot_copy.start()

    if comm:
        barrier = pltpu.get_barrier_semaphore()
        around = [
            device(z, yy, xx, cc)
            for yy, xx, cc in (
                (y, x, 1 - core),
                (y, 1 - x, core),
                (1 - y, x, core),
                (1 - y, 1 - x, core),
                (y, 1 - x, 1 - core),
                (1 - y, x, 1 - core),
                (1 - y, 1 - x, 1 - core),
            )
        ]
        greeted = around + [device(plane(step), y, x, core) for step in range(1, planes)]
        for target in greeted:
            pl.semaphore_signal(barrier, inc=1, device_id=target, device_id_type=MESH)
        for copy in weight_copies:
            copy.wait()
        for u in range(UNITS):
            unit[u, z, y, x, :, mine] = normed[held(2, u)].astype(bf16)
        pl.semaphore_wait(barrier, len(greeted))
    else:
        unit_copy = pltpu.make_async_copy(whole_hbm, unit, local_sem.at[4])
        unit_copy.start()
        unit_copy.wait()

    gather()
    sums[...] = jnp.zeros_like(sums)
    up_sums[...] = jnp.zeros_like(up_sums)
    if comm:
        squares[...] = jnp.zeros_like(squares)
    own_copy.wait()

    def fold_vectors():
        target = vec_sum.at[0] if comm else vectors
        target[pl.ds(0, 8), :] = jnp.sum(sums[...], axis=1)
        folded = jnp.sum(up_sums[...], axis=1)
        for u in range(4):
            for c in range(2):
                target[pl.ds(8 + c * 2 + u // 2, 1), pl.ds((u % 2) * HALF, HALF)] = folded[
                    u : u + 1, c * HALF : (c + 1) * HALF
                ]

    if comm:
        place = (y * 2 + x) * 2 + core
        vec_targets = (sibling, device(z, y, 1 - x, core), device(z, 1 - y, x, core))

        def vec_copy(stage):
            return remote(
                vec_sum.at[stage],
                vec_in.at[stage],
                vec_send.at[stage],
                vec_recv.at[stage],
                vec_targets[stage],
            )

        def vec_plane(step):
            return remote(
                vec_sum.at[3],
                vec_z_in.at[z],
                vec_send.at[2 + step],
                vec_recv.at[2 + step],
                device(plane(step), y, x, core),
            )

        def vec_start():
            vec_copy(0).start()

        def vec_step(stage):
            vec_copy(stage).wait_recv()
            vec_sum[stage + 1] = vec_sum[stage] + vec_in[stage]
            if stage < 2:
                vec_copy(stage + 1).start()
            else:
                vec_z_in[z] = vec_sum[3]
                for step in range(1, planes):
                    vec_plane(step).start()

        def vec_done():
            for step in range(1, planes):
                vec_plane(step).wait_recv()
            total = vec_z_in[0]
            for zz in range(1, planes):
                total = total + vec_z_in[zz]
            vectors[...] = total

        def vec_sent():
            for stage in range(3):
                vec_copy(stage).wait_send()
            for step in range(1, planes):
                vec_plane(step).wait_send()

        def square_near(step):
            piece = square_in.at[place]
            return remote(piece, piece, square_send.at[step], square_recv.at[step], around[step])

        def square_far(step):
            piece = square_in.at[8 + z]
            sem = len(around) - 1 + step
            return remote(
                piece, piece, square_send.at[sem], square_recv.at[sem], device(plane(step), y, x, core)
            )

        def exchange_squares():
            square_in[place] = jnp.sum(squares[...], axis=1)
            for step in range(len(around)):
                square_near(step).start()
            for step in range(len(around)):
                square_near(step).wait_recv()
            square_in[8 + z] = jnp.sum(square_in[pl.ds(0, 8)], axis=0)
            for step in range(1, planes):
                square_far(step).start()
            for step in range(1, planes):
                square_far(step).wait_recv()
            total = jnp.sum(square_in[pl.ds(8, planes)], axis=0)
            norms[...] = jnp.broadcast_to(
                jnp.sqrt(jnp.sum(total, axis=1, keepdims=True)), norms.shape
            )
            for step in range(len(around)):
                square_near(step).wait_send()
            for step in range(1, planes):
                square_far(step).wait_send()

    def probs_out(t):
        return pltpu.make_async_copy(probs.at[t % chains], probs_hbm.at[t], probs_sem.at[t % chains])

    def probs_back(t):
        return pltpu.make_async_copy(probs_hbm.at[t], probs.at[t % chains], probs_sem.at[t % chains])

    position = lax.broadcasted_iota(jnp.int32, (1, length), 1)

    for g in range(3):
        gather()
        ready(g)
        bias = jnp.concatenate(
            [
                piece
                for c in range(2)
                for piece in (
                    small[pl.ds(0, 1), pl.ds(c * HALF + g * LANES, LANES)],
                    jnp.zeros((1, LANES), f32),
                    small[pl.ds(1, 1), pl.ds(c * HALF + g * LANES, LANES)],
                )
            ],
            axis=1,
        )
        lane = lax.broadcasted_iota(jnp.int32, (1, WIDE), 1) % HALF
        scale = jnp.where(lane < LANES, HEAD ** (-0.5), 1.0)

        def project(r):
            rows = tile(r, count)
            for j in range(3):
                cols = pl.ds(j * QUAD, QUAD)
                part = slice(j * QUAD, (j + 1) * QUAD)
                packed[g, rows, cols] = (
                    (nn(own[rows, :], unit_cols(g, cols)) + bias[:, part]).astype(bf16).astype(f32)
                    * scale[:, part]
                ).astype(bf16)

        loop(1, project)
        gather()

        def attend(chain):
            t = g * chains + chain
            if g:
                probs_out(t - chains).wait()
            rows = pl.ds(chain * length, length)
            here = packed.at[g]
            queries = spread_heads(pair(here, rows, 0))
            keys = pair(here, rows, LANES)
            values = pair(here, rows, 2 * LANES)
            limit = lengths[chain // per_micro, chain % per_micro]
            scores = jnp.where(position < limit, nt(queries, keys), MASKED_SCORE)
            peak = jnp.max(scores, axis=1, keepdims=True)
            exponent = jnp.exp(scores - peak)
            total = jnp.sum(exponent, axis=1, keepdims=True)
            low = (exponent * (1.0 / total)).astype(bf16)
            mixed = pick_heads(nn(low, values), length).astype(bf16)
            return rows, low, mixed

        def attend_some(some):
            for chain, (rows, low, mixed) in [(chain, attend(chain)) for chain in some]:
                probs[chain, :, pl.ds(0, length)] = low
                if g < 2:
                    probs_out(g * chains + chain).start()
                put_pair(context, rows, g * LANES, mixed)

        attend_some(range(chains // 2))
        gather()
        attend_some(range(chains // 2, chains))
        gather()

    gather()
    ready(3)

    def mid(r):
        rows = tile(r, count)
        back[rows, :] = nt(context[rows, :], weights(3))

    loop(1, mid)
    gather()

    def first_norm(r):
        rows = tile(r, BLOCK)
        value = own[rows, :].astype(f32) + back[rows, :] + small[pl.ds(2, 1), :]
        center = value - mean_last(value)
        root = lax.rsqrt(mean_last(center * center) + NORM_EPS)
        scaled = center * root
        normed[rows, :] = scaled
        inverse[rows, :] = root
        first[rows, :] = (scaled * small[pl.ds(3, 1), :] + small[pl.ds(4, 1), :]).astype(bf16)

    loop(count // BLOCK, first_norm)
    gather()

    def up(u):
        gather()
        ready(4 + u)
        bias = jnp.concatenate(
            [
                small[pl.ds(8 + c * 2 + u // 2, 1), pl.ds((u % 2) * HALF, HALF)]
                for c in range(2)
            ],
            axis=1,
        )

        def block(r):
            rows = tile(r, count)
            for j in range(3):
                cols = pl.ds(j * QUAD, QUAD)
                upper = nn(first[rows, :], unit_cols(4 + u, cols)) + bias[:, j * QUAD : (j + 1) * QUAD]
                share = 0.5 + 0.5 * lax.erf(upper * 0.7071067811865476)
                hidden[u, rows, cols] = (upper * share).astype(bf16)
                slope[u, rows, cols] = (
                    share + upper * (0.3989422804014327 * jnp.exp(-0.5 * upper * upper))
                ).astype(bf16)

        loop(1, block)

    def down(u):
        gather()
        ready(8 + u)

        def block(r):
            rows = tile(r, count)
            term = nt(hidden[u, rows, :], weights(8 + u))
            back[rows, :] = term if u == 0 else back[rows, :] + term

        loop(1, block)

    for u in range(4):
        up(u)
        gather()
    for u in range(4):
        down(u)
        gather()
    if comm:
        for u in range(UNITS):
            ag_sent(u)
    cot_copy.wait()

    def flip(source, target):
        for j in range(WIDE // LANES):
            cols = pl.ds(j * LANES, LANES)
            target[cols, :] = source[:, cols].T

    def second_norm(r):
        rows = tile(r, BLOCK)
        value = (
            normed[rows, :] * small[pl.ds(3, 1), :]
            + small[pl.ds(4, 1), :]
            + back[rows, :]
            + small[pl.ds(5, 1), :]
        )
        center = value - mean_last(value)
        root = lax.rsqrt(mean_last(center * center) + NORM_EPS)
        scaled = center * root
        upstream = cot[rows, :].astype(f32)
        cot[rows, :] = (scaled * small[pl.ds(6, 1), :] + small[pl.ds(7, 1), :]).astype(bf16)
        gained = upstream * small[pl.ds(6, 1), :]
        grad = (gained - mean_last(gained) - scaled * mean_last(gained * scaled)) * root
        back[rows, :] = grad
        low = grad.astype(bf16)
        own[rows, :] = low
        sums[5] += fold_rows(low.astype(f32))
        sums[6] += fold_rows(upstream * scaled)
        sums[7] += fold_rows(upstream)

    loop(count // BLOCK, second_norm)
    out_copy.start()
    flip(own, flip_a)
    flip(first, flip_b)

    def outer(u, flipped, source):
        def block(r):
            part = nn(flipped[...], source[...]).astype(bf16)
            unit[G_SLOT.get(u, u)] = part.reshape(unit.shape[1:])

        loop(1, block)

    for u in range(4):

        def block(r, u=u):
            rows = tile(r, count)
            for j in range(3):
                cols = pl.ds(j * QUAD, QUAD)
                low = (nn(own[rows, :], unit_cols(8 + u, cols)) * slope[u, rows, cols].astype(f32)).astype(
                    bf16
                )
                slope[u, rows, cols] = low
                up_sums[u, :, cols] += fold_rows(low.astype(f32))

        loop(1, block)
        reduce()
        outer(8 + u, flip_a, hidden.at[u])
        if comm:
            rs_start(8 + u)
        reduce()

        def gather_first(r, u=u):
            rows = tile(r, count)
            back[rows, :] += nt(slope[u, rows, :], weights(4 + u))

        loop(1, gather_first)
        reduce()
        outer(4 + u, flip_b, slope.at[u])
        if comm:
            rs_start(4 + u)
        reduce()

    def first_back(r):
        rows = tile(r, BLOCK)
        upstream = back[rows, :]
        scaled = normed[rows, :]
        gained = upstream * small[pl.ds(3, 1), :]
        grad = (gained - mean_last(gained) - scaled * mean_last(gained * scaled)) * inverse[rows, :]
        back[rows, :] = grad
        low = grad.astype(bf16)
        own[rows, :] = low
        sums[2] += fold_rows(low.astype(f32))
        sums[3] += fold_rows(upstream * scaled)
        sums[4] += fold_rows(upstream)

    loop(count // BLOCK, first_back)
    if comm:
        step_copies = held_copies(0) + held_copies(1) + held_copies(2)
        for copy in step_copies:
            copy.start()
    reduce()
    out_copy.wait()
    flip(own, flip_a)
    if comm:
        for copy in step_copies:
            copy.wait()
    reduce()

    def mid_back(r):
        rows = tile(r, count)
        for j in range(3):
            cols = pl.ds(j * QUAD, QUAD)
            cot[rows, cols] = nn(own[rows, :], unit_cols(3, cols)).astype(bf16)

    loop(1, mid_back)
    reduce()
    outer(3, flip_a, context)
    if comm:
        rs_start(3)
    own_again = pltpu.make_async_copy(tokens_hbm, own, local_sem.at[0])
    own_again.start()
    reduce()
    own_again.wait()
    flip(own, flip_b)
    reduce()

    for g in (2, 1, 0):
        grads = hidden.at[g]

        def attend_back(chain):
            if g < 2:
                probs_back(g * chains + chain).wait()
            rows = pl.ds(chain * length, length)
            here = packed.at[g]
            queries = spread_heads(pair(here, rows, 0))
            keys = pair(here, rows, LANES)
            values = pair(here, rows, 2 * LANES)
            d_context = spread_heads(pair(cot, rows, g * LANES))
            low = probs[chain, :, pl.ds(0, length)]
            wide = low.astype(f32)
            d_probs = nt(d_context, values)
            inner = jnp.sum(wide * d_probs, axis=1, keepdims=True)
            d_scores = (wide * (d_probs - inner)).astype(bf16)
            d_queries = (pick_heads(nn(d_scores, keys), length) * HEAD ** (-0.5)).astype(bf16)
            d_keys = tn(d_scores, queries).astype(bf16)
            d_values = tn(low, d_context).astype(bf16)
            return rows, d_queries, d_keys, d_values

        def back_some(some):
            results = [(chain, attend_back(chain)) for chain in some]
            for chain, (rows, d_queries, d_keys, d_values) in results:
                put_pair(grads, rows, 0, d_queries)
                put_pair(grads, rows, LANES, d_keys)
                put_pair(grads, rows, 2 * LANES, d_values)
                if g:
                    probs_back((g - 1) * chains + chain).start()
            for row, place_of in ((0, 1), (1, 3)):
                folded = sum(fold_rows(result[place_of].astype(f32)) for _, result in results)
                for c in range(2):
                    cols = pl.ds(c * HALF + g * LANES, LANES)
                    sums[row, :, cols] += folded[:, c * LANES : (c + 1) * LANES]

        back_some(range(chains // 2))
        reduce()
        back_some(range(chains // 2, chains))
        if g == 0:
            fold_vectors()
            if comm:
                vec_start()
        reduce()
        if comm:
            rs_sent(G_SLOT[g])
        outer(g, flip_b, grads)
        if comm:
            rs_start(g)
        reduce()

    for g in (2, 1, 0):

        def tokens_back(r):
            rows = tile(r, count)
            back[rows, :] += nt(hidden[g, rows, :], weights(g))

        loop(1, tokens_back)
        if g == 0:
            back_copy.start()
        reduce()
        if comm:
            vec_step(2 - g)

    if comm:
        reduce()
        vec_done()
        exchange_squares()
        for u in range(UNITS):
            if u not in G_SLOT.values():
                rs_sent(u)
            shard_copy(u).wait()
        vec_sent()
    else:
        whole_out = pltpu.make_async_copy(unit, shard, local_sem.at[4])
        whole_out.start()
        whole_out.wait()
    back_copy.wait()


def run_layer(tokens, lengths, cotangent, weights, moments, small, ranks):
    rows_here = weights[1].shape[0]
    width = small.shape[1]
    flat = tokens.reshape(-1, width)
    count = flat.shape[0]
    chains = lengths.size
    length = tokens.shape[2]
    comm = gathers_inside(ranks, rows_here)
    planes = ranks // 4 if comm else 4
    padded = -(-length // LANES) * LANES
    steps = planes - 1
    unit_shape = (UNITS, planes, 2, 2, width // (planes * 4), WIDE)
    vmem = pl.BlockSpec(memory_space=pltpu.VMEM)
    hbm = pl.BlockSpec(memory_space=pl.ANY)
    operands = [lengths, flat, cotangent.reshape(-1, width), small, *weights]
    in_specs = [pl.BlockSpec(memory_space=pltpu.SMEM), hbm, hbm, vmem] + [hbm] * 4
    if not comm:
        shard = jnp.stack([unit_part(weights, u) for u in range(UNITS)]).astype(bf16)
        whole = lax.all_gather(shard, "dp", axis=1, tiled=True)
        whole = lax.all_gather(whole, "mp", axis=2, tiled=True)
        operands.append(whole.reshape(unit_shape))
        in_specs.append(hbm)
    else:
        operands += moments
        in_specs += [hbm] * 8
    shard_shape = (UNITS, rows_here, HALF)
    out_shape = [
        jax.ShapeDtypeStruct((count, width), bf16),
        jax.ShapeDtypeStruct((count, width), f32),
        jax.ShapeDtypeStruct(shard_shape, f32) if comm else jax.ShapeDtypeStruct(unit_shape, bf16),
        jax.ShapeDtypeStruct(small.shape, f32),
        jax.ShapeDtypeStruct((2 * chains, 4 * length, padded), bf16),
    ]
    out_specs = [hbm, hbm, hbm, vmem, hbm]
    if comm:
        out_shape.insert(4, jax.ShapeDtypeStruct((8, LANES), f32))
        out_specs.insert(4, vmem)
    scratch = [
        pltpu.VMEM((count, width), f32),
        pltpu.VMEM(unit_shape, bf16),
        pltpu.VMEM((3, count, WIDE), bf16),
        pltpu.VMEM((count, width), bf16),
        pltpu.VMEM((count, width), f32),
        pltpu.VMEM((count, 1), f32),
        pltpu.VMEM((count, width), bf16),
        pltpu.VMEM((4, count, WIDE), bf16),
        pltpu.VMEM((4, count, WIDE), bf16),
        pltpu.VMEM((count, width), bf16),
        pltpu.VMEM((count, width), bf16),
        pltpu.VMEM((width, count), bf16),
        pltpu.VMEM((width, count), bf16),
        pltpu.VMEM((chains, 4 * length, padded), bf16),
        pltpu.VMEM((8, 8, width), f32),
        pltpu.VMEM((4, 8, WIDE), f32),
        pltpu.SemaphoreType.DMA((5,)),
        pltpu.SemaphoreType.DMA((chains,)),
    ]
    params = dict(vmem_limit_bytes=64 * 2**20 - 2**16)
    if comm:
        scratch += [
            pltpu.VMEM((UNITS, planes, 2, 2, rows_here, HALF), bf16),
            pltpu.VMEM((UNITS, planes, rows_here, HALF), bf16),
            pltpu.VMEM((UNITS, 2, planes, rows_here, HALF), bf16),
            pltpu.VMEM((UNITS, steps, rows_here, HALF), bf16),
            pltpu.VMEM((8, 8, LANES), f32),
            pltpu.VMEM((8 + planes, 8, LANES), f32),
            pltpu.VMEM((4,) + small.shape, f32),
            pltpu.VMEM((3,) + small.shape, f32),
            pltpu.VMEM((planes,) + small.shape, f32),
            pltpu.SemaphoreType.DMA((UNITS, 2 * steps + 4)),
            pltpu.SemaphoreType.DMA((UNITS, 2 * steps + 4)),
            pltpu.SemaphoreType.DMA((UNITS, 2 * steps + 4)),
            pltpu.SemaphoreType.DMA((UNITS, 2 * steps + 4)),
            pltpu.SemaphoreType.DMA((3 + steps,)),
            pltpu.SemaphoreType.DMA((3 + steps,)),
            pltpu.SemaphoreType.DMA((7 + steps,)),
            pltpu.SemaphoreType.DMA((7 + steps,)),
            pltpu.SemaphoreType.DMA((3, UNITS + 6)),
            pltpu.SemaphoreType.DMA((UNITS,)),
        ]
        params.update(collective_id=0, has_side_effects=True)
    out, back, shard, vectors, *rest = pl.pallas_call(
        functools.partial(main_kernel, comm),
        out_shape=out_shape,
        in_specs=in_specs,
        out_specs=out_specs,
        scratch_shapes=scratch,
        compiler_params=pltpu.CompilerParams(**params),
    )(*operands)
    norms = rest[0] if comm else None
    if not comm:
        summed = shard.reshape(UNITS, width, 2, HALF).astype(f32)
        summed = lax.psum_scatter(summed, "mp", scatter_dimension=2, tiled=True)
        summed = lax.psum_scatter(
            summed.reshape(UNITS, width, HALF), "dp", scatter_dimension=1, tiled=True
        )
        shard = summed
    return out, back, shard, vectors, norms


def gathers_inside(ranks, rows_here):
    return ranks % 4 == 0 and rows_here % 16 == 0


def put_unit(refs, u, values):
    if u < 3:
        for k in range(3):
            refs[0][k, :, pl.ds(u * LANES, LANES)] = values[:, k * LANES : (k + 1) * LANES]
    elif u == 3:
        refs[1][...] = values
    else:
        refs[2 + (u - 4) // 4][:, pl.ds((u % 4) * HALF, HALF)] = values


def step_kernel(*refs):
    out_in, back_in, shard, vectors, norms = refs[:5]
    weights, moments = refs[5:9], refs[9:17]
    small, small_first, small_second = refs[17:20]
    outs = refs[20:-3]
    out_held, back_held, sem = refs[-3:]
    inward = [
        pltpu.make_async_copy(out_in, out_held, sem.at[0]),
        pltpu.make_async_copy(back_in, back_held, sem.at[1]),
    ]
    outward = [
        pltpu.make_async_copy(out_held, outs[0], sem.at[2]),
        pltpu.make_async_copy(back_held, outs[1], sem.at[3]),
    ]
    for copy in inward:
        copy.start()
    grads, firsts, seconds, news, lows = (
        [outs[2 + 5 * m + which] for m in range(4)] for which in range(5)
    )
    for u in range(UNITS):
        if u in (4, 8):
            inward[u // 4 - 1].wait()
            outward[u // 4 - 1].start()
        gradient = shard[u]
        first_new, second_new, direction = adam_moments(
            gradient, unit_part(moments[:4], u), unit_part(moments[4:], u)
        )
        weight = unit_part(weights, u)
        which = MATRIX_OF[u]
        rate = RATE_MATRIX * (norms[which : which + 1, :1] / norms[4 + which : 5 + which, :1])
        renewed = weight - rate * (direction + DECAY_RATE * weight)
        put_unit(grads, u, gradient)
        put_unit(firsts, u, first_new)
        put_unit(seconds, u, second_new)
        put_unit(news, u, renewed)
        put_unit(lows, u, renewed.astype(bf16))
    vector_grad = vectors[...]
    first_new, second_new, direction = adam_moments(vector_grad, small_first[...], small_second[...])
    outs[22][...] = vector_grad
    outs[23][...] = first_new
    outs[24][...] = second_new
    outs[25][...] = small[...] - RATE_VECTOR * direction
    for row in range(2):
        for m in range(4):
            outs[26][pl.ds(row, 1), pl.ds(m, 1)] = norms[4 * row + m : 4 * row + m + 1, :1]
    for copy in outward:
        copy.wait()


def run_step(out, back, shard, vectors, norms, weights, moments, small, small_first, small_second):
    vmem = pl.BlockSpec(memory_space=pltpu.VMEM)
    hbm = pl.BlockSpec(memory_space=pl.ANY)
    out_shape = [jax.ShapeDtypeStruct(out.shape, bf16), jax.ShapeDtypeStruct(back.shape, f32)]
    for weight in weights:
        out_shape += [jax.ShapeDtypeStruct(weight.shape, f32)] * 4
        out_shape += [jax.ShapeDtypeStruct(weight.shape, bf16)]
    out_shape += [jax.ShapeDtypeStruct(small.shape, f32)] * 4
    out_shape += [jax.ShapeDtypeStruct((2, 4), f32)]
    return pl.pallas_call(
        step_kernel,
        out_shape=out_shape,
        in_specs=[hbm, hbm] + [vmem] * 18,
        out_specs=[hbm, hbm] + [vmem] * 25,
        scratch_shapes=[
            pltpu.VMEM(out.shape, bf16),
            pltpu.VMEM(back.shape, f32),
            pltpu.SemaphoreType.DMA((4,)),
        ],
        compiler_params=pltpu.CompilerParams(vmem_limit_bytes=64 * 2**20 - 2**16),
    )(out, back, shard, vectors, norms, *weights, *moments, small, small_first, small_second)


def body(
    ranks,
    tokens,
    lengths,
    cotangent,
    attn_in,
    attn_out,
    ffn_in,
    ffn_out,
    attn_in_first,
    attn_in_second,
    attn_out_first,
    attn_out_second,
    ffn_in_first,
    ffn_in_second,
    ffn_out_first,
    ffn_out_second,
    small,
    small_first,
    small_second,
):
    weights = (attn_in.transpose(1, 0, 2), attn_out.T, ffn_in, ffn_out.T)
    all_moments = (
        attn_in_first.transpose(1, 0, 2),
        attn_out_first.T,
        ffn_in_first,
        ffn_out_first.T,
        attn_in_second.transpose(1, 0, 2),
        attn_out_second.T,
        ffn_in_second,
        ffn_out_second.T,
    )
    output, tokens_grad, shard, vectors, norms = run_layer(
        tokens, lengths, cotangent, weights, all_moments, small, ranks
    )
    if norms is not None:
        results = run_step(
            output,
            tokens_grad,
            shard,
            vectors,
            norms,
            weights,
            all_moments,
            small,
            small_first,
            small_second,
        )
        results = list(results)
        results[0] = results[0].reshape(tokens.shape)
        results[1] = results[1].reshape(tokens.shape)
        for i in range(5):
            results[2 + i] = results[2 + i].transpose(1, 0, 2)
            results[7 + i] = results[7 + i].T
            results[17 + i] = results[17 + i].T
        return tuple(results)
    output, tokens_grad = output.reshape(tokens.shape), tokens_grad.reshape(tokens.shape)
    rows = attn_in.shape[0]
    grad_in = jnp.concatenate([shard[g].reshape(rows, 3, LANES) for g in range(3)], axis=2)
    grad_mid = shard[3].T
    grad_up = jnp.concatenate([shard[4 + u] for u in range(4)], axis=1)
    grad_down = jnp.concatenate([shard[8 + u].T for u in range(4)], axis=0)
    matrices = (
        (attn_in, grad_in, attn_in_first, attn_in_second),
        (attn_out, grad_mid, attn_out_first, attn_out_second),
        (ffn_in, grad_up, ffn_in_first, ffn_in_second),
        (ffn_out, grad_down, ffn_out_first, ffn_out_second),
    )
    moments = [adam_moments(entry[1], entry[2], entry[3]) for entry in matrices]
    headings = [moments[i][2] + DECAY_RATE * matrices[i][0] for i in range(4)]
    weight_squares = jnp.stack([jnp.sum(entry[0] * entry[0]) for entry in matrices])
    step_squares = jnp.stack([jnp.sum(heading * heading) for heading in headings])
    vector_grad, weight_sums, step_sums = lax.psum(
        (vectors, weight_squares, step_squares), ("dp", "mp")
    )
    weight_norms = jnp.sqrt(weight_sums)
    step_norms = jnp.sqrt(step_sums)
    results = [output, tokens_grad]
    for i in range(4):
        weight = matrices[i][0]
        renewed = weight - RATE_MATRIX * (weight_norms[i] / step_norms[i]) * headings[i]
        results.extend(
            [matrices[i][1], moments[i][0], moments[i][1], renewed, renewed.astype(bf16)]
        )
    small_first_new, small_second_new, small_direction = adam_moments(
        vector_grad, small_first, small_second
    )
    small_new = small - RATE_VECTOR * small_direction
    results.extend(
        [
            vector_grad,
            small_first_new,
            small_second_new,
            small_new,
            jnp.stack((weight_norms, step_norms)),
        ]
    )
    return tuple(results)


def solution(mesh):
    chains = P(None, ("dp", "mp"), None, None)
    rows_three = P("dp", None, "mp")
    rows_two = P("dp", "mp")
    columns = P("mp", "dp")
    whole = P()
    return jax.shard_map(
        functools.partial(body, mesh.shape["dp"]),
        mesh=mesh,
        in_specs=(
            chains,
            P(None, ("dp", "mp")),
            chains,
            rows_three,
            columns,
            rows_two,
            columns,
            rows_three,
            rows_three,
            columns,
            columns,
            rows_two,
            rows_two,
            columns,
            columns,
            whole,
            whole,
            whole,
        ),
        out_specs=(
            (chains, chains)
            + (rows_three,) * 5
            + (columns,) * 5
            + (rows_two,) * 5
            + (columns,) * 5
            + (whole,) * 5
        ),
        check_vma=False,
    )
```

```python
import functools

import jax
import jax.numpy as jnp
from jax import lax
from jax.experimental import pallas as pl
from jax.experimental.pallas import tpu as pltpu
from jax.sharding import PartitionSpec as P

HEAD = 64
STEP = 10
NORM_EPS = 1e-05
RATE_MATRIX = 0.3
RATE_VECTOR = 0.2
BETA_FIRST = 0.9
BETA_SECOND = 0.999
ADAM_EPS = 1e-06
DECAY_RATE = 0.01
MASKED_SCORE = -1000000000.0

MESH = pl.DeviceIdType.MESH
bf16, f32 = jnp.bfloat16, jnp.float32
UNITS = 12
HALF = 384
MATRIX_OF = (0, 0, 0, 1, 2, 2, 2, 2, 3, 3, 3, 3)
WIDE = 768
LANES = 128
QUAD = 256
BLOCK = 192
G_SLOT = {2: 9, 1: 10, 0: 8}
PLANES, LINES, DIAGONAL, SIBLING, OWN, DONE, SHARDS = range(7)
SPLIT_GATHER = (5, 7, 9, 10)
SPLIT_SUMS = (8, 4, 9, 5)
GATHER = (
    ((PLANES, 0), (PLANES, 1), (PLANES, 2),),
    ((LINES, 0), (PLANES, 3), (LINES, 1), (PLANES, 4), (DIAGONAL, 0), (PLANES, 5), (LINES, 2), (PLANES, 6), (DIAGONAL, 1), (PLANES, 7), (LINES, 3), (PLANES, 8), (SIBLING, 0), (PLANES, 9), (SHARDS, 5), (PLANES, 10),),
    (),
    ((DIAGONAL, 2), (PLANES, 11), (LINES, 4),),
    ((SHARDS, 7), (SIBLING, 1), (LINES, 5),),
    (),
    ((DIAGONAL, 3),),
    ((SHARDS, 9), (SHARDS, 10), (LINES, 6),),
    ((SIBLING, 2), (LINES, 7),),
    (),
    ((DIAGONAL, 4),),
    ((LINES, 8),),
    ((SIBLING, 3), (LINES, 9),),
    (),
    ((DIAGONAL, 6),),
    ((DIAGONAL, 5),),
    ((SIBLING, 4), (LINES, 10),),
    (),
    ((DIAGONAL, 8), (LINES, 11), (SIBLING, 6), (DIAGONAL, 7), (SIBLING, 5),),
    (),
    (),
    ((SIBLING, 8), (DIAGONAL, 9),),
    ((DIAGONAL, 10), (DIAGONAL, 11), (SIBLING, 7),),
    ((SIBLING, 9),),
    (),
    ((SIBLING, 10),),
    (),
    ((SIBLING, 11),),
    (),
    (),
    (),
    (),
)
REDUCE = (
    (),
    (),
    (),
    ((OWN, 8),),
    ((OWN, 4),),
    (),
    ((DIAGONAL, 8), (OWN, 9), (LINES, 8),),
    ((DIAGONAL, 4),),
    ((LINES, 4), (OWN, 5),),
    ((SHARDS, 8), (DIAGONAL, 9),),
    ((LINES, 9), (OWN, 10),),
    ((DIAGONAL, 5),),
    ((LINES, 5), (OWN, 6),),
    ((SHARDS, 4), (DIAGONAL, 10),),
    ((OWN, 11),),
    ((DIAGONAL, 6),),
    ((OWN, 7), (SHARDS, 9),),
    ((LINES, 10), (DONE, 8), (DONE, 4),),
    ((DIAGONAL, 11),),
    (),
    (),
    ((SHARDS, 5), (DIAGONAL, 7), (LINES, 6), (OWN, 3),),
    ((DONE, 9),),
    ((LINES, 11), (DONE, 5),),
    ((LINES, 7), (OWN, 2), (DONE, 10), (DIAGONAL, 3),),
    ((DONE, 6),),
    ((DIAGONAL, 2),),
    ((OWN, 1), (DONE, 11), (LINES, 3),),
    ((LINES, 2), (DONE, 7),),
    ((DIAGONAL, 1),),
    ((OWN, 0), (DONE, 3),),
    ((LINES, 1),),
    ((DIAGONAL, 0), (DONE, 2),),
    ((DONE, 1), (LINES, 0), (DONE, 0),),
)


def nn(left, right):
    return lax.dot_general(left, right, (((1,), (0,)), ((), ())), preferred_element_type=f32)


def nt(left, right):
    return lax.dot_general(left, right, (((1,), (1,)), ((), ())), preferred_element_type=f32)


def tn(left, right):
    return lax.dot_general(left, right, (((0,), (0,)), ((), ())), preferred_element_type=f32)


def tile(index, size):
    if isinstance(index, int):
        return pl.ds(index * size, size)
    return pl.ds(pl.multiple_of(index * size, size), size)


def loop(count, body):
    def step(index, carry):
        body(index)
        return carry

    if count == 1:
        body(0)
    else:
        lax.fori_loop(0, count, step, 0)


def mean_last(values):
    return jnp.sum(values, axis=-1, keepdims=True) * (1.0 / values.shape[-1])


def fold_rows(values):
    return jnp.sum(values.reshape(values.shape[0] // 8, 8, values.shape[1]), axis=0)


def fold_tile(values):
    folded = fold_rows(values)
    return sum(folded[:, c : c + LANES] for c in range(0, folded.shape[1], LANES))


def unit_part(refs, u):
    if u < 3:
        return jnp.concatenate([refs[0][k, :, pl.ds(u * LANES, LANES)] for k in range(3)], axis=1)
    if u == 3:
        return refs[1][...]
    return refs[2 + (u - 4) // 4][:, pl.ds((u % 4) * HALF, HALF)]


def adam_moments(gradient, first_moment, second_moment):
    first_new = BETA_FIRST * first_moment + (1.0 - BETA_FIRST) * gradient
    second_new = BETA_SECOND * second_moment + (1.0 - BETA_SECOND) * gradient * gradient
    direction = (
        first_new
        / (1.0 - BETA_FIRST**STEP)
        / (jnp.sqrt(second_new / (1.0 - BETA_SECOND**STEP)) + ADAM_EPS)
    )
    return (first_new, second_new, direction)


def head_lane():
    return lax.broadcasted_iota(jnp.int32, (1, QUAD), 1) // HEAD


def spread_heads(values):
    lane = head_lane()
    zero = jnp.zeros_like(values)
    return jnp.concatenate([jnp.where(lane == head, values, zero) for head in range(4)], axis=0)


def pick_heads(values, length):
    lane = head_lane()
    result = values[:length]
    for head in range(1, 4):
        result = jnp.where(lane == head, values[head * length : (head + 1) * length], result)
    return result


def lanes(offset, size=LANES):
    if isinstance(offset, int):
        return pl.ds(offset, size)
    return pl.ds(pl.multiple_of(offset, LANES), size)


def pair(ref, rows, offset):
    return jnp.concatenate([ref[rows, lanes(offset)], ref[rows, lanes(HALF + offset)]], axis=1)


def put_pair(ref, rows, offset, values):
    ref[rows, lanes(offset)] = values[:, :LANES]
    ref[rows, lanes(HALF + offset)] = values[:, LANES:]


def main_kernel(
    comm,
    lengths,
    tokens_hbm,
    cot_hbm,
    small,
    w_in,
    w_mid,
    w_up,
    w_down,
    *rest,
):
    if comm:
        *moments_hbm, out_hbm, back_hbm, shard, vectors, norms, probs_hbm = rest[:14]
        rest = rest[14:]
    else:
        whole_hbm, out_hbm, back_hbm, shard, vectors, probs_hbm = rest[:6]
        rest = rest[6:]
    (
        back,
        unit,
        packed,
        context,
        normed,
        inverse,
        first,
        hidden,
        slope,
        own,
        cot,
        flip_a,
        flip_b,
        probs,
        sums,
        up_sums,
        local_sem,
        probs_sem,
        *rest,
    ) = rest
    if comm:
        sib_in, diag_in, line_in, z_in, *rest = rest
        squares, square_in, vec_sum, vec_in, vec_z_in = rest[:5]
        send, recv, rs_send, rs_recv, vec_send, vec_recv, square_send, square_recv, held_sem, shard_sem = rest[5:]
    micro, per_micro = lengths.shape
    chains = micro * per_micro
    length = own.shape[0] // chains
    count = own.shape[0]

    planes = unit.shape[1]
    if comm:
        rank = lax.axis_index("dp")
        core = lax.axis_index("mp")
        z, y, x = rank // 4, (rank // 2) % 2, rank % 2
        mine = pl.ds(pl.multiple_of(core * HALF, HALF), HALF)
        other = pl.ds(pl.multiple_of((1 - core) * HALF, HALF), HALF)

        def device(zz, yy, xx, cc):
            return (zz * 4 + yy * 2 + xx, cc)

        y1, x1 = jnp.where(core == 0, y, 1 - y), jnp.where(core == 0, 1 - x, x)
        y2, x2 = jnp.where(core == 0, 1 - y, y), jnp.where(core == 0, x, 1 - x)
        near = device(z, y1, x1, core)
        next_ = device(z, y2, x2, core)
        sibling = device(z, y, x, 1 - core)

        def plane(step):
            return lax.rem(z + step, planes)

        def plane_back(step):
            return lax.rem(z + planes - step, planes)

        def remote(src, dst, ssem, rsem, target):
            return pltpu.make_async_remote_copy(
                src_ref=src,
                dst_ref=dst,
                send_sem=ssem,
                recv_sem=rsem,
                device_id=target,
                device_id_type=MESH,
            )

        LINE = planes - 1

        def gz(u, step):
            piece = unit.at[u, z, y, x, :, mine]
            return remote(
                piece, piece, send.at[u, step - 1], recv.at[u, step - 1], device(plane(step), y, x, core)
            )

        def gline(u, which):
            piece = unit.at[u, :, y, x, :, mine]
            return remote(
                piece,
                piece,
                send.at[u, LINE + which],
                recv.at[u, LINE + which],
                near if which else next_,
            )

        def gdiag(u):
            piece = unit.at[u, :, y2, x2, :, mine]
            return remote(piece, piece, send.at[u, LINE + 2], recv.at[u, LINE + 2], near)

        def gsib(u):
            piece = unit.at[u, :, :, :, :, mine]
            return remote(piece, piece, send.at[u, LINE + 3], recv.at[u, LINE + 3], sibling)

        def gshard(u):
            piece = unit.at[u, z, y, x, :, mine]
            return remote(piece, piece, send.at[u, LINE], recv.at[u, LINE], next_)

        def gz_next(u, step):
            piece = unit.at[u, z, y2, x2, :, mine]
            sem = LINE + 3 + step
            return remote(piece, piece, send.at[u, sem], recv.at[u, sem], device(plane(step), y, x, core))

        def ag_z(u):
            for step in range(1, planes):
                gz(u, step).start()
            if u in SPLIT_GATHER:
                gshard(u).start()

        def ag_shard(u):
            gshard(u).wait_recv()
            for step in range(1, planes):
                gz_next(u, step).start()

        def ag_line(u):
            for step in range(1, planes):
                gz(u, step).wait_recv()
            if u not in SPLIT_GATHER:
                gline(u, 0).start()
            gline(u, 1).start()

        def ag_diag(u):
            if u in SPLIT_GATHER:
                for step in range(1, planes):
                    gz_next(u, step).wait_recv()
            else:
                gline(u, 0).wait_recv()
            gdiag(u).start()

        def ag_sib(u):
            gline(u, 1).wait_recv()
            gdiag(u).wait_recv()
            gsib(u).start()

        def ag_ready(u):
            gsib(u).wait_recv()

        def ag_sent(u):
            for step in range(1, planes):
                gz(u, step).wait_send()
            if u in SPLIT_GATHER:
                gshard(u).wait_send()
                for step in range(1, planes):
                    gz_next(u, step).wait_send()
            else:
                gline(u, 0).wait_send()
            gline(u, 1).wait_send()
            gdiag(u).wait_send()
            gsib(u).wait_send()

        def slot(u):
            return G_SLOT.get(u, u)

        def rsib(u, place=None):
            place = slot(u) if place is None else place
            return remote(
                unit.at[place, :, :, :, :, other], sib_in.at[u], rs_send.at[u, 0], rs_recv.at[u, 0], sibling
            )

        def rdiag(u):
            return remote(
                unit.at[slot(u), :, 1 - y, 1 - x, :, mine],
                diag_in.at[u],
                rs_send.at[u, 1],
                rs_recv.at[u, 1],
                near,
            )

        def rline(u, which):
            yy, xx = (y2, x2) if which else (y1, x1)
            return remote(
                unit.at[slot(u), :, yy, xx, :, mine],
                line_in.at[u, which],
                rs_send.at[u, 2 + which],
                rs_recv.at[u, 2 + which],
                next_ if which else near,
            )

        def rz(u, step):
            return remote(
                unit.at[slot(u), plane(step), y, x, :, mine],
                z_in.at[u, step - 1],
                rs_send.at[u, 3 + step],
                rs_recv.at[u, 3 + step],
                device(plane(step), y, x, core),
            )

        def rz_next(u, step):
            sem = 3 + planes + step - 1
            return remote(
                unit.at[slot(u), plane(step), y2, x2, :, mine],
                line_in.at[u, 1, step - 1],
                rs_send.at[u, sem],
                rs_recv.at[u, sem],
                device(plane(step), y, x, core),
            )

        def rshard(u):
            return remote(
                unit.at[slot(u), z, y2, x2, :, mine],
                line_in.at[u, 1, planes - 1],
                rs_send.at[u, 3],
                rs_recv.at[u, 3],
                next_,
            )

        def rs_start(u, place=None):
            rsib(u, place).start()

        def rs_own(u):
            rsib(u).wait_recv()

            def add(zz):
                for yy in range(2):
                    for xx in range(2):
                        unit[slot(u), zz, yy, xx, :, mine] = (
                            unit[slot(u), zz, yy, xx, :, mine].astype(f32) + sib_in[u, zz, yy, xx].astype(f32)
                        ).astype(bf16)

            loop(planes, add)
            rdiag(u).start()
            rline(u, 0).start()

        def rs_diag(u):
            rdiag(u).wait_recv()

            def add(zz):
                unit[slot(u), zz, y2, x2, :, mine] = (
                    unit[slot(u), zz, y2, x2, :, mine].astype(f32) + diag_in[u, zz].astype(f32)
                ).astype(bf16)

            loop(planes, add)
            if u in SPLIT_SUMS:
                for step in range(1, planes):
                    rz_next(u, step).start()
            else:
                rline(u, 1).start()

        def rs_shard(u):
            total = unit[slot(u), z, y2, x2, :, mine].astype(f32)
            for step in range(1, planes):
                rz_next(u, step).wait_recv()
                total = total + line_in[u, 1, step - 1].astype(f32)
            unit[slot(u), z, y2, x2, :, mine] = total.astype(bf16)
            rshard(u).start()

        def rs_line(u):
            rline(u, 0).wait_recv()
            if u not in SPLIT_SUMS:
                rline(u, 1).wait_recv()

            def add(zz):
                total = unit[slot(u), zz, y, x, :, mine].astype(f32) + line_in[u, 0, zz].astype(f32)
                if u not in SPLIT_SUMS:
                    total = total + line_in[u, 1, zz].astype(f32)
                unit[slot(u), zz, y, x, :, mine] = total.astype(bf16)

            loop(planes, add)
            for step in range(1, planes):
                rz(u, step).start()

        def rs_done(u):
            total = unit[slot(u), z, y, x, :, mine].astype(f32)
            for step in range(1, planes):
                rz(u, step).wait_recv()
                total = total + z_in[u, step - 1].astype(f32)
            if u in SPLIT_SUMS:
                rshard(u).wait_recv()
                total = total + line_in[u, 1, planes - 1].astype(f32)
            _, _, direction = adam_moments(total, normed[held(0, u)], normed[held(1, u)])
            weight = normed[held(2, u)]
            normed[held(0, u)] = total
            shard_copy(u).start()
            heading = direction + DECAY_RATE * weight
            which = MATRIX_OF[u]
            squares[which] += fold_tile(weight * weight)
            squares[4 + which] += fold_tile(heading * heading)

        def held(which, u):
            rows = normed.shape[0] // 20
            row = (which * UNITS + u) // 2 * rows
            return pl.ds(row, rows), pl.ds((u % 2) * HALF, HALF)

        def held_copies(which):
            matrices = (moments_hbm[:4], moments_hbm[4:], (w_in, w_mid, w_up, w_down))[which]
            copies = []
            for u in range(UNITS):
                rows, cols = held(which, u)
                if u < 3:
                    pairs = [
                        (
                            matrices[0].at[k, :, pl.ds(u * LANES, LANES)],
                            normed.at[rows, pl.ds(cols.start + k * LANES, LANES)],
                        )
                        for k in range(3)
                    ]
                elif u == 3:
                    pairs = [(matrices[1], normed.at[rows, cols])]
                else:
                    piece = matrices[2 + (u - 4) // 4].at[:, pl.ds((u % 4) * HALF, HALF)]
                    pairs = [(piece, normed.at[rows, cols])]
                for source, target in pairs:
                    sem = held_sem.at[which, len(copies)]
                    copies.append(pltpu.make_async_copy(source, target, sem))
            return copies

        def shard_copy(u):
            return pltpu.make_async_copy(normed.at[held(0, u)], shard.at[u], shard_sem.at[u])

        def rs_sent(u):
            rsib(u).wait_send()
            rdiag(u).wait_send()
            rline(u, 0).wait_send()
            if u in SPLIT_SUMS:
                rshard(u).wait_send()
                for step in range(1, planes):
                    rz_next(u, step).wait_send()
            else:
                rline(u, 1).wait_send()
            for step in range(1, planes):
                rz(u, step).wait_send()

    if comm:
        gathers = {
            PLANES: ag_z,
            SHARDS: ag_shard,
            LINES: ag_line,
            DIAGONAL: ag_diag,
            SIBLING: ag_sib,
        }
        sums_of = {
            OWN: rs_own,
            DIAGONAL: rs_diag,
            SHARDS: rs_shard,
            LINES: rs_line,
            DONE: rs_done,
        }
    gather_plan, reduce_plan = iter(GATHER), iter(REDUCE)

    def planned(plan, kinds):
        def run():
            for kind, u in next(plan):
                if comm:
                    kinds[kind](u)

        return run

    kinds = (gathers, sums_of) if comm else ({}, {})
    gather, reduce = planned(gather_plan, kinds[0]), planned(reduce_plan, kinds[1])

    def staged(plan, turns, stages, extra=None):
        sends = [[next(plan) for _ in stages] for _ in range(turns)]
        kinds_here = kinds[0] if plan is gather_plan else kinds[1]

        def turn(i):
            for s, stage in enumerate(stages):
                stage(i)
                for k in range(turns):
                    more = extra.get((k, s)) if extra else None
                    if comm and (sends[k][s] or more):

                        @pl.when(i == k)
                        def _(k=k, s=s, more=more):
                            for kind, u in sends[k][s]:
                                kinds_here[kind](u)
                            if more:
                                more()

        loop(turns, turn)

    def nothing(i):
        pass

    def ready(u):
        if comm:
            ag_ready(u)

    def weights(u):
        return unit[u].reshape(WIDE, WIDE)

    def unit_cols(u, columns):
        return unit[u, :, :, :, :, columns].reshape(WIDE, columns.size)

    own_copy = pltpu.make_async_copy(tokens_hbm, own, local_sem.at[0])
    cot_copy = pltpu.make_async_copy(cot_hbm, cot, local_sem.at[1])
    out_copy = pltpu.make_async_copy(cot, out_hbm, local_sem.at[2])
    back_copy = pltpu.make_async_copy(back, back_hbm, local_sem.at[3])
    if comm:
        weight_copies = held_copies(2)
        for copy in weight_copies:
            copy.start()
    own_copy.start()
    cot_copy.start()

    if comm:
        barrier = pltpu.get_barrier_semaphore()
        around = [
            device(z, yy, xx, cc)
            for yy, xx, cc in (
                (y, x, 1 - core),
                (y, 1 - x, core),
                (1 - y, x, core),
                (1 - y, 1 - x, core),
                (y, 1 - x, 1 - core),
                (1 - y, x, 1 - core),
                (1 - y, 1 - x, 1 - core),
            )
        ]
        greeted = around + [device(plane(step), y, x, core) for step in range(1, planes)]
        for target in greeted:
            pl.semaphore_signal(barrier, inc=1, device_id=target, device_id_type=MESH)
        for copy in weight_copies:
            copy.wait()
        for u in range(UNITS):
            unit[u, z, y, x, :, mine] = normed[held(2, u)].astype(bf16)
        pl.semaphore_wait(barrier, len(greeted))
    else:
        unit_copy = pltpu.make_async_copy(whole_hbm, unit, local_sem.at[4])
        unit_copy.start()
        unit_copy.wait()

    gather()
    sums[...] = jnp.zeros_like(sums)
    up_sums[...] = jnp.zeros_like(up_sums)
    if comm:
        squares[...] = jnp.zeros_like(squares)
    own_copy.wait()

    def fold_vectors():
        target = vec_sum.at[0] if comm else vectors
        target[pl.ds(0, 8), :] = jnp.sum(sums[...], axis=1)
        folded = jnp.sum(up_sums[...], axis=1)
        for u in range(4):
            for c in range(2):
                target[pl.ds(8 + c * 2 + u // 2, 1), pl.ds((u % 2) * HALF, HALF)] = folded[
                    u : u + 1, c * HALF : (c + 1) * HALF
                ]

    if comm:
        place = (y * 2 + x) * 2 + core
        vec_targets = (sibling, device(z, y, 1 - x, core), device(z, 1 - y, x, core))

        def vec_copy(stage):
            return remote(
                vec_sum.at[stage],
                vec_in.at[stage],
                vec_send.at[stage],
                vec_recv.at[stage],
                vec_targets[stage],
            )

        def vec_plane(step):
            return remote(
                vec_sum.at[3],
                vec_z_in.at[z],
                vec_send.at[2 + step],
                vec_recv.at[2 + step],
                device(plane(step), y, x, core),
            )

        def vec_start():
            vec_copy(0).start()

        def vec_step(stage):
            vec_copy(stage).wait_recv()
            vec_sum[stage + 1] = vec_sum[stage] + vec_in[stage]
            if stage < 2:
                vec_copy(stage + 1).start()
            else:
                vec_z_in[z] = vec_sum[3]
                for step in range(1, planes):
                    vec_plane(step).start()

        def vec_done():
            for step in range(1, planes):
                vec_plane(step).wait_recv()
            total = vec_z_in[0]
            for zz in range(1, planes):
                total = total + vec_z_in[zz]
            vectors[...] = total

        def vec_sent():
            for stage in range(3):
                vec_copy(stage).wait_send()
            for step in range(1, planes):
                vec_plane(step).wait_send()

        def square_near(step):
            piece = square_in.at[place]
            return remote(piece, piece, square_send.at[step], square_recv.at[step], around[step])

        def square_far(step):
            piece = square_in.at[8 + z]
            sem = len(around) - 1 + step
            return remote(
                piece, piece, square_send.at[sem], square_recv.at[sem], device(plane(step), y, x, core)
            )

        def exchange_squares():
            square_in[place] = jnp.sum(squares[...], axis=1)
            for step in range(len(around)):
                square_near(step).start()
            for step in range(len(around)):
                square_near(step).wait_recv()
            square_in[8 + z] = jnp.sum(square_in[pl.ds(0, 8)], axis=0)
            for step in range(1, planes):
                square_far(step).start()
            for step in range(1, planes):
                square_far(step).wait_recv()
            total = jnp.sum(square_in[pl.ds(8, planes)], axis=0)
            norms[...] = jnp.broadcast_to(
                jnp.sqrt(jnp.sum(total, axis=1, keepdims=True)), norms.shape
            )
            for step in range(len(around)):
                square_near(step).wait_send()
            for step in range(1, planes):
                square_far(step).wait_send()

    def probs_out(t, chain):
        return pltpu.make_async_copy(probs.at[chain], probs_hbm.at[t], probs_sem.at[chain])

    def probs_back(t, chain):
        return pltpu.make_async_copy(probs_hbm.at[t], probs.at[chain], probs_sem.at[chain])

    position = lax.broadcasted_iota(jnp.int32, (1, length), 1)

    def project(g):
        ready(g)
        bias = jnp.concatenate(
            [
                piece
                for c in range(2)
                for piece in (
                    small[pl.ds(0, 1), lanes(c * HALF + g * LANES)],
                    jnp.zeros((1, LANES), f32),
                    small[pl.ds(1, 1), lanes(c * HALF + g * LANES)],
                )
            ],
            axis=1,
        )
        lane = lax.broadcasted_iota(jnp.int32, (1, WIDE), 1) % HALF
        scale = jnp.where(lane < LANES, HEAD ** (-0.5), 1.0)
        for j in range(3):
            cols = pl.ds(j * QUAD, QUAD)
            part = slice(j * QUAD, (j + 1) * QUAD)
            packed[g, :, cols] = (
                (nn(own[...], unit_cols(g, cols)) + bias[:, part]).astype(bf16).astype(f32)
                * scale[:, part]
            ).astype(bf16)

    def attend(g, chain):
        rows = pl.ds(chain * length, length)
        here = packed.at[g]
        queries = spread_heads(pair(here, rows, 0))
        keys = pair(here, rows, LANES)
        values = pair(here, rows, 2 * LANES)
        limit = lengths[chain // per_micro, chain % per_micro]
        scores = jnp.where(position < limit, nt(queries, keys), MASKED_SCORE)
        peak = jnp.max(scores, axis=1, keepdims=True)
        exponent = jnp.exp(scores - peak)
        total = jnp.sum(exponent, axis=1, keepdims=True)
        low = (exponent * (1.0 / total)).astype(bf16)
        mixed = pick_heads(nn(low, values), length).astype(bf16)
        return rows, low, mixed

    def attend_some(some):
        def stage(g):
            @pl.when(g > 0)
            def _():
                for chain in some:
                    probs_out((g - 1) * chains + chain, chain).wait()

            for chain, (rows, low, mixed) in [(chain, attend(g, chain)) for chain in some]:
                probs[chain, :, pl.ds(0, length)] = low
                put_pair(context, rows, g * LANES, mixed)

            @pl.when(g < 2)
            def _():
                for chain in some:
                    probs_out(g * chains + chain, chain).start()

        return stage

    halves = (range(chains // 2), range(chains // 2, chains))
    staged(gather_plan, 3, [nothing, project] + [attend_some(some) for some in halves])

    gather()
    ready(3)

    def mid(r):
        rows = tile(r, count)
        back[rows, :] = nt(context[rows, :], weights(3))

    loop(1, mid)
    gather()

    def first_norm(r):
        rows = tile(r, BLOCK)
        value = own[rows, :].astype(f32) + back[rows, :] + small[pl.ds(2, 1), :]
        center = value - mean_last(value)
        root = lax.rsqrt(mean_last(center * center) + NORM_EPS)
        scaled = center * root
        normed[rows, :] = scaled
        inverse[rows, :] = root
        first[rows, :] = (scaled * small[pl.ds(3, 1), :] + small[pl.ds(4, 1), :]).astype(bf16)

    loop(count // BLOCK, first_norm)
    gather()

    def up(u):
        ready(4 + u)
        bias = jnp.concatenate(
            [
                small[pl.ds(8 + c * 2 + u // 2, 1), lanes((u % 2) * HALF, HALF)]
                for c in range(2)
            ],
            axis=1,
        )
        for j in range(3):
            cols = pl.ds(j * QUAD, QUAD)
            upper = nn(first[...], unit_cols(4 + u, cols)) + bias[:, j * QUAD : (j + 1) * QUAD]
            share = 0.5 + 0.5 * lax.erf(upper * 0.7071067811865476)
            hidden[u, :, cols] = (upper * share).astype(bf16)
            slope[u, :, cols] = (
                share + upper * (0.3989422804014327 * jnp.exp(-0.5 * upper * upper))
            ).astype(bf16)

    def down(u):
        ready(8 + u)
        back[...] += nt(hidden[u], weights(8 + u))

    staged(gather_plan, 4, [nothing, up])
    back[...] = jnp.zeros_like(back)
    staged(gather_plan, 4, [nothing, down])
    if comm:
        for u in range(UNITS):
            ag_sent(u)
    cot_copy.wait()

    def flip(source, target):
        for j in range(WIDE // LANES):
            cols = pl.ds(j * LANES, LANES)
            target[cols, :] = source[:, cols].T

    def second_norm(r):
        rows = tile(r, BLOCK)
        value = (
            normed[rows, :] * small[pl.ds(3, 1), :]
            + small[pl.ds(4, 1), :]
            + back[rows, :]
            + small[pl.ds(5, 1), :]
        )
        center = value - mean_last(value)
        root = lax.rsqrt(mean_last(center * center) + NORM_EPS)
        scaled = center * root
        upstream = cot[rows, :].astype(f32)
        cot[rows, :] = (scaled * small[pl.ds(6, 1), :] + small[pl.ds(7, 1), :]).astype(bf16)
        gained = upstream * small[pl.ds(6, 1), :]
        grad = (gained - mean_last(gained) - scaled * mean_last(gained * scaled)) * root
        back[rows, :] = grad
        low = grad.astype(bf16)
        own[rows, :] = low
        sums[5] += fold_rows(low.astype(f32))
        sums[6] += fold_rows(upstream * scaled)
        sums[7] += fold_rows(upstream)

    loop(count // BLOCK, second_norm)
    out_copy.start()
    flip(own, flip_a)
    flip(first, flip_b)

    def outer(place, flipped, source):
        part = nn(flipped[...], source[...]).astype(bf16)
        unit[place] = part.reshape(unit.shape[1:])

    def hidden_back(u):
        for j in range(3):
            cols = pl.ds(j * QUAD, QUAD)
            low = (nn(own[...], unit_cols(8 + u, cols)) * slope[u, :, cols].astype(f32)).astype(bf16)
            slope[u, :, cols] = low
            up_sums[u, :, cols] += fold_rows(low.astype(f32))

    def down_sums(u):
        outer(8 + u, flip_a, hidden.at[u])
        if comm:
            rs_start(8 + u, 8 + u)

    def first_part(u):
        back[...] += nt(slope[u], weights(4 + u))

    def up_sums_out(u):
        outer(4 + u, flip_b, slope.at[u])
        if comm:
            rs_start(4 + u, 4 + u)

    staged(reduce_plan, 4, [hidden_back, down_sums, first_part, up_sums_out])

    def first_back(r):
        rows = tile(r, BLOCK)
        upstream = back[rows, :]
        scaled = normed[rows, :]
        gained = upstream * small[pl.ds(3, 1), :]
        grad = (gained - mean_last(gained) - scaled * mean_last(gained * scaled)) * inverse[rows, :]
        back[rows, :] = grad
        low = grad.astype(bf16)
        own[rows, :] = low
        sums[2] += fold_rows(low.astype(f32))
        sums[3] += fold_rows(upstream * scaled)
        sums[4] += fold_rows(upstream)

    loop(count // BLOCK, first_back)
    if comm:
        step_copies = held_copies(0) + held_copies(1) + held_copies(2)
        for copy in step_copies:
            copy.start()
    reduce()
    out_copy.wait()
    flip(own, flip_a)
    if comm:
        for copy in step_copies:
            copy.wait()
    reduce()

    for j in range(3):
        cols = pl.ds(j * QUAD, QUAD)
        cot[:, cols] = nn(own[...], unit_cols(3, cols)).astype(bf16)
    reduce()
    outer(3, flip_a, context)
    if comm:
        rs_start(3)
    own_again = pltpu.make_async_copy(tokens_hbm, own, local_sem.at[0])
    own_again.start()
    reduce()
    own_again.wait()
    flip(own, flip_b)
    reduce()

    def attend_back(g, chain):
        rows = pl.ds(chain * length, length)
        here = packed.at[g]
        queries = spread_heads(pair(here, rows, 0))
        keys = pair(here, rows, LANES)
        values = pair(here, rows, 2 * LANES)
        d_context = spread_heads(pair(cot, rows, g * LANES))
        low = probs[chain, :, pl.ds(0, length)]
        wide = low.astype(f32)
        d_probs = nt(d_context, values)
        inner = jnp.sum(wide * d_probs, axis=1, keepdims=True)
        d_scores = (wide * (d_probs - inner)).astype(bf16)
        d_queries = (pick_heads(nn(d_scores, keys), length) * HEAD ** (-0.5)).astype(bf16)
        d_keys = tn(d_scores, queries).astype(bf16)
        d_values = tn(low, d_context).astype(bf16)
        return rows, d_queries, d_keys, d_values

    def back_some(some):
        def stage(i):
            g = 2 - i
            grads = hidden.at[g]

            @pl.when(g < 2)
            def _():
                for chain in some:
                    probs_back(g * chains + chain, chain).wait()

            results = [attend_back(g, chain) for chain in some]
            for rows, d_queries, d_keys, d_values in results:
                put_pair(grads, rows, 0, d_queries)
                put_pair(grads, rows, LANES, d_keys)
                put_pair(grads, rows, 2 * LANES, d_values)
            for row, place_of in ((0, 1), (1, 3)):
                folded = sum(fold_rows(result[place_of].astype(f32)) for result in results)
                for c in range(2):
                    cols = lanes(c * HALF + g * LANES)
                    sums[row, :, cols] += folded[:, c * LANES : (c + 1) * LANES]

            @pl.when(g > 0)
            def _():
                for chain in some:
                    probs_back((g - 1) * chains + chain, chain).start()

        return stage

    def head_sums(i):
        g = 2 - i
        place = 8 + (i + 1) % 3
        outer(place, flip_b, hidden.at[g])
        if comm:
            rs_start(g, place)

    def vectors_out():
        fold_vectors()
        vec_start()

    def freed(k):
        def run():
            rs_sent(G_SLOT[2 - k])
            if k == 2:
                vectors_out()

        return run

    def tokens_back(i):
        g = 2 - i
        back[...] += nt(hidden[g], weights(g))

    def tokens_out():
        back_copy.start()
        vec_step(2)

    staged(
        reduce_plan,
        3,
        [back_some(some) for some in halves] + [head_sums],
        {(k, 1): freed(k) for k in range(3)} if comm else None,
    )
    staged(
        reduce_plan,
        3,
        [tokens_back],
        {(0, 0): lambda: vec_step(0), (1, 0): lambda: vec_step(1), (2, 0): tokens_out}
        if comm
        else None,
    )
    if not comm:
        fold_vectors()
        back_copy.start()

    if comm:
        reduce()
        vec_done()
        exchange_squares()
        for u in range(UNITS):
            if u not in G_SLOT.values():
                rs_sent(u)
            shard_copy(u).wait()
        vec_sent()
    else:
        whole_out = pltpu.make_async_copy(unit, shard, local_sem.at[4])
        whole_out.start()
        whole_out.wait()
    back_copy.wait()


def run_layer(tokens, lengths, cotangent, weights, moments, small, ranks):
    rows_here = weights[1].shape[0]
    width = small.shape[1]
    flat = tokens.reshape(-1, width)
    count = flat.shape[0]
    chains = lengths.size
    length = tokens.shape[2]
    comm = gathers_inside(ranks, rows_here)
    planes = ranks // 4 if comm else 4
    padded = -(-length // LANES) * LANES
    steps = planes - 1
    unit_shape = (UNITS, planes, 2, 2, width // (planes * 4), WIDE)
    vmem = pl.BlockSpec(memory_space=pltpu.VMEM)
    hbm = pl.BlockSpec(memory_space=pl.ANY)
    operands = [lengths, flat, cotangent.reshape(-1, width), small, *weights]
    in_specs = [pl.BlockSpec(memory_space=pltpu.SMEM), hbm, hbm, vmem] + [hbm] * 4
    if not comm:
        shard = jnp.stack([unit_part(weights, u) for u in range(UNITS)]).astype(bf16)
        whole = lax.all_gather(shard, "dp", axis=1, tiled=True)
        whole = lax.all_gather(whole, "mp", axis=2, tiled=True)
        operands.append(whole.reshape(unit_shape))
        in_specs.append(hbm)
    else:
        operands += moments
        in_specs += [hbm] * 8
    shard_shape = (UNITS, rows_here, HALF)
    out_shape = [
        jax.ShapeDtypeStruct((count, width), bf16),
        jax.ShapeDtypeStruct((count, width), f32),
        jax.ShapeDtypeStruct(shard_shape, f32) if comm else jax.ShapeDtypeStruct(unit_shape, bf16),
        jax.ShapeDtypeStruct(small.shape, f32),
        jax.ShapeDtypeStruct((2 * chains, 4 * length, padded), bf16),
    ]
    out_specs = [hbm, hbm, hbm, vmem, hbm]
    if comm:
        out_shape.insert(4, jax.ShapeDtypeStruct((8, LANES), f32))
        out_specs.insert(4, vmem)
    scratch = [
        pltpu.VMEM((count, width), f32),
        pltpu.VMEM(unit_shape, bf16),
        pltpu.VMEM((3, count, WIDE), bf16),
        pltpu.VMEM((count, width), bf16),
        pltpu.VMEM((count, width), f32),
        pltpu.VMEM((count, 1), f32),
        pltpu.VMEM((count, width), bf16),
        pltpu.VMEM((4, count, WIDE), bf16),
        pltpu.VMEM((4, count, WIDE), bf16),
        pltpu.VMEM((count, width), bf16),
        pltpu.VMEM((count, width), bf16),
        pltpu.VMEM((width, count), bf16),
        pltpu.VMEM((width, count), bf16),
        pltpu.VMEM((chains, 4 * length, padded), bf16),
        pltpu.VMEM((8, 8, width), f32),
        pltpu.VMEM((4, 8, WIDE), f32),
        pltpu.SemaphoreType.DMA((5,)),
        pltpu.SemaphoreType.DMA((chains,)),
    ]
    params = dict(vmem_limit_bytes=64 * 2**20 - 2**16)
    if comm:
        scratch += [
            pltpu.VMEM((UNITS, planes, 2, 2, rows_here, HALF), bf16),
            pltpu.VMEM((UNITS, planes, rows_here, HALF), bf16),
            pltpu.VMEM((UNITS, 2, planes, rows_here, HALF), bf16),
            pltpu.VMEM((UNITS, steps, rows_here, HALF), bf16),
            pltpu.VMEM((8, 8, LANES), f32),
            pltpu.VMEM((8 + planes, 8, LANES), f32),
            pltpu.VMEM((4,) + small.shape, f32),
            pltpu.VMEM((3,) + small.shape, f32),
            pltpu.VMEM((planes,) + small.shape, f32),
            pltpu.SemaphoreType.DMA((UNITS, 2 * steps + 4)),
            pltpu.SemaphoreType.DMA((UNITS, 2 * steps + 4)),
            pltpu.SemaphoreType.DMA((UNITS, 2 * steps + 4)),
            pltpu.SemaphoreType.DMA((UNITS, 2 * steps + 4)),
            pltpu.SemaphoreType.DMA((3 + steps,)),
            pltpu.SemaphoreType.DMA((3 + steps,)),
            pltpu.SemaphoreType.DMA((7 + steps,)),
            pltpu.SemaphoreType.DMA((7 + steps,)),
            pltpu.SemaphoreType.DMA((3, UNITS + 6)),
            pltpu.SemaphoreType.DMA((UNITS,)),
        ]
        params.update(collective_id=0, has_side_effects=True)
    out, back, shard, vectors, *rest = pl.pallas_call(
        functools.partial(main_kernel, comm),
        out_shape=out_shape,
        in_specs=in_specs,
        out_specs=out_specs,
        scratch_shapes=scratch,
        compiler_params=pltpu.CompilerParams(**params),
    )(*operands)
    norms = rest[0] if comm else None
    if not comm:
        summed = shard.reshape(UNITS, width, 2, HALF).astype(f32)
        summed = lax.psum_scatter(summed, "mp", scatter_dimension=2, tiled=True)
        summed = lax.psum_scatter(
            summed.reshape(UNITS, width, HALF), "dp", scatter_dimension=1, tiled=True
        )
        shard = summed
    return out, back, shard, vectors, norms


def gathers_inside(ranks, rows_here):
    return ranks % 4 == 0 and rows_here % 16 == 0


def put_unit(refs, u, values):
    if u < 3:
        for k in range(3):
            refs[0][k, :, pl.ds(u * LANES, LANES)] = values[:, k * LANES : (k + 1) * LANES]
    elif u == 3:
        refs[1][...] = values
    else:
        refs[2 + (u - 4) // 4][:, pl.ds((u % 4) * HALF, HALF)] = values


def step_kernel(*refs):
    out_in, back_in, shard, vectors, norms = refs[:5]
    weights, moments = refs[5:9], refs[9:17]
    small, small_first, small_second = refs[17:20]
    outs = refs[20:-3]
    out_held, back_held, sem = refs[-3:]
    inward = [
        pltpu.make_async_copy(out_in, out_held, sem.at[0]),
        pltpu.make_async_copy(back_in, back_held, sem.at[1]),
    ]
    outward = [
        pltpu.make_async_copy(out_held, outs[0], sem.at[2]),
        pltpu.make_async_copy(back_held, outs[1], sem.at[3]),
    ]
    for copy in inward:
        copy.start()
    grads, firsts, seconds, news, lows = (
        [outs[2 + 5 * m + which] for m in range(4)] for which in range(5)
    )
    for u in range(UNITS):
        if u in (4, 8):
            inward[u // 4 - 1].wait()
            outward[u // 4 - 1].start()
        gradient = shard[u]
        first_new, second_new, direction = adam_moments(
            gradient, unit_part(moments[:4], u), unit_part(moments[4:], u)
        )
        weight = unit_part(weights, u)
        which = MATRIX_OF[u]
        rate = RATE_MATRIX * (norms[which : which + 1, :1] / norms[4 + which : 5 + which, :1])
        renewed = weight - rate * (direction + DECAY_RATE * weight)
        put_unit(grads, u, gradient)
        put_unit(firsts, u, first_new)
        put_unit(seconds, u, second_new)
        put_unit(news, u, renewed)
        put_unit(lows, u, renewed.astype(bf16))
    vector_grad = vectors[...]
    first_new, second_new, direction = adam_moments(vector_grad, small_first[...], small_second[...])
    outs[22][...] = vector_grad
    outs[23][...] = first_new
    outs[24][...] = second_new
    outs[25][...] = small[...] - RATE_VECTOR * direction
    for row in range(2):
        for m in range(4):
            outs[26][pl.ds(row, 1), pl.ds(m, 1)] = norms[4 * row + m : 4 * row + m + 1, :1]
    for copy in outward:
        copy.wait()


def run_step(out, back, shard, vectors, norms, weights, moments, small, small_first, small_second):
    vmem = pl.BlockSpec(memory_space=pltpu.VMEM)
    hbm = pl.BlockSpec(memory_space=pl.ANY)
    out_shape = [jax.ShapeDtypeStruct(out.shape, bf16), jax.ShapeDtypeStruct(back.shape, f32)]
    for weight in weights:
        out_shape += [jax.ShapeDtypeStruct(weight.shape, f32)] * 4
        out_shape += [jax.ShapeDtypeStruct(weight.shape, bf16)]
    out_shape += [jax.ShapeDtypeStruct(small.shape, f32)] * 4
    out_shape += [jax.ShapeDtypeStruct((2, 4), f32)]
    return pl.pallas_call(
        step_kernel,
        out_shape=out_shape,
        in_specs=[hbm, hbm] + [vmem] * 18,
        out_specs=[hbm, hbm] + [vmem] * 25,
        scratch_shapes=[
            pltpu.VMEM(out.shape, bf16),
            pltpu.VMEM(back.shape, f32),
            pltpu.SemaphoreType.DMA((4,)),
        ],
        compiler_params=pltpu.CompilerParams(vmem_limit_bytes=64 * 2**20 - 2**16),
    )(out, back, shard, vectors, norms, *weights, *moments, small, small_first, small_second)


def body(
    ranks,
    tokens,
    lengths,
    cotangent,
    attn_in,
    attn_out,
    ffn_in,
    ffn_out,
    attn_in_first,
    attn_in_second,
    attn_out_first,
    attn_out_second,
    ffn_in_first,
    ffn_in_second,
    ffn_out_first,
    ffn_out_second,
    small,
    small_first,
    small_second,
):
    weights = (attn_in.transpose(1, 0, 2), attn_out.T, ffn_in, ffn_out.T)
    all_moments = (
        attn_in_first.transpose(1, 0, 2),
        attn_out_first.T,
        ffn_in_first,
        ffn_out_first.T,
        attn_in_second.transpose(1, 0, 2),
        attn_out_second.T,
        ffn_in_second,
        ffn_out_second.T,
    )
    output, tokens_grad, shard, vectors, norms = run_layer(
        tokens, lengths, cotangent, weights, all_moments, small, ranks
    )
    if norms is not None:
        results = run_step(
            output,
            tokens_grad,
            shard,
            vectors,
            norms,
            weights,
            all_moments,
            small,
            small_first,
            small_second,
        )
        results = list(results)
        results[0] = results[0].reshape(tokens.shape)
        results[1] = results[1].reshape(tokens.shape)
        for i in range(5):
            results[2 + i] = results[2 + i].transpose(1, 0, 2)
            results[7 + i] = results[7 + i].T
            results[17 + i] = results[17 + i].T
        return tuple(results)
    output, tokens_grad = output.reshape(tokens.shape), tokens_grad.reshape(tokens.shape)
    rows = attn_in.shape[0]
    grad_in = jnp.concatenate([shard[g].reshape(rows, 3, LANES) for g in range(3)], axis=2)
    grad_mid = shard[3].T
    grad_up = jnp.concatenate([shard[4 + u] for u in range(4)], axis=1)
    grad_down = jnp.concatenate([shard[8 + u].T for u in range(4)], axis=0)
    matrices = (
        (attn_in, grad_in, attn_in_first, attn_in_second),
        (attn_out, grad_mid, attn_out_first, attn_out_second),
        (ffn_in, grad_up, ffn_in_first, ffn_in_second),
        (ffn_out, grad_down, ffn_out_first, ffn_out_second),
    )
    moments = [adam_moments(entry[1], entry[2], entry[3]) for entry in matrices]
    headings = [moments[i][2] + DECAY_RATE * matrices[i][0] for i in range(4)]
    weight_squares = jnp.stack([jnp.sum(entry[0] * entry[0]) for entry in matrices])
    step_squares = jnp.stack([jnp.sum(heading * heading) for heading in headings])
    vector_grad, weight_sums, step_sums = lax.psum(
        (vectors, weight_squares, step_squares), ("dp", "mp")
    )
    weight_norms = jnp.sqrt(weight_sums)
    step_norms = jnp.sqrt(step_sums)
    results = [output, tokens_grad]
    for i in range(4):
        weight = matrices[i][0]
        renewed = weight - RATE_MATRIX * (weight_norms[i] / step_norms[i]) * headings[i]
        results.extend(
            [matrices[i][1], moments[i][0], moments[i][1], renewed, renewed.astype(bf16)]
        )
    small_first_new, small_second_new, small_direction = adam_moments(
        vector_grad, small_first, small_second
    )
    small_new = small - RATE_VECTOR * small_direction
    results.extend(
        [
            vector_grad,
            small_first_new,
            small_second_new,
            small_new,
            jnp.stack((weight_norms, step_norms)),
        ]
    )
    return tuple(results)


def solution(mesh):
    chains = P(None, ("dp", "mp"), None, None)
    rows_three = P("dp", None, "mp")
    rows_two = P("dp", "mp")
    columns = P("mp", "dp")
    whole = P()
    return jax.shard_map(
        functools.partial(body, mesh.shape["dp"]),
        mesh=mesh,
        in_specs=(
            chains,
            P(None, ("dp", "mp")),
            chains,
            rows_three,
            columns,
            rows_two,
            columns,
            rows_three,
            rows_three,
            columns,
            columns,
            rows_two,
            rows_two,
            columns,
            columns,
            whole,
            whole,
            whole,
        ),
        out_specs=(
            (chains, chains)
            + (rows_three,) * 5
            + (columns,) * 5
            + (rows_two,) * 5
            + (columns,) * 5
            + (whole,) * 5
        ),
        check_vma=False,
    )
```

```python
import functools

import jax
import jax.numpy as jnp
from jax import lax
from jax.experimental import pallas as pl
from jax.experimental.pallas import tpu as pltpu
from jax.sharding import PartitionSpec as P

HEAD = 64
STEP = 10
NORM_EPS = 1e-05
RATE_MATRIX = 0.3
RATE_VECTOR = 0.2
BETA_FIRST = 0.9
BETA_SECOND = 0.999
ADAM_EPS = 1e-06
DECAY_RATE = 0.01
MASKED_SCORE = -1000000000.0

MESH = pl.DeviceIdType.MESH
bf16, f32 = jnp.bfloat16, jnp.float32
UNITS = 12
HALF = 384
MATRIX_OF = (0, 0, 0, 1, 2, 2, 2, 2, 3, 3, 3, 3)
WIDE = 768
LANES = 128
QUAD = 256
BLOCK = 192
G_SLOT = {2: 9, 1: 10, 0: 8}
PLANES, LINES, DIAGONAL, SIBLING, OWN, DONE, SHARDS = range(7)
SPLIT_GATHER = (5, 7, 9, 10)
SPLIT_SUMS = (8, 4, 9, 5)
GATHER = (
    ((PLANES, 0), (PLANES, 1), (PLANES, 2),),
    ((LINES, 0), (PLANES, 3), (LINES, 1), (PLANES, 4), (DIAGONAL, 0), (PLANES, 5), (LINES, 2), (PLANES, 6), (DIAGONAL, 1), (PLANES, 7), (LINES, 3), (PLANES, 8), (SIBLING, 0), (PLANES, 9), (SHARDS, 5), (PLANES, 10),),
    (),
    ((DIAGONAL, 2), (PLANES, 11), (LINES, 4),),
    ((SHARDS, 7), (SIBLING, 1), (LINES, 5),),
    (),
    ((DIAGONAL, 3),),
    ((SHARDS, 9), (SHARDS, 10), (LINES, 6),),
    ((SIBLING, 2), (LINES, 7),),
    (),
    ((DIAGONAL, 4),),
    ((LINES, 8),),
    ((SIBLING, 3), (LINES, 9),),
    (),
    ((DIAGONAL, 6),),
    ((DIAGONAL, 5),),
    ((SIBLING, 4), (LINES, 10),),
    (),
    ((DIAGONAL, 8), (LINES, 11), (SIBLING, 6), (DIAGONAL, 7), (SIBLING, 5),),
    (),
    (),
    ((SIBLING, 8), (DIAGONAL, 9),),
    ((DIAGONAL, 10), (DIAGONAL, 11), (SIBLING, 7),),
    ((SIBLING, 9),),
    (),
    ((SIBLING, 10),),
    (),
    ((SIBLING, 11),),
    (),
    (),
    (),
    (),
)
REDUCE = (
    (),
    (),
    (),
    ((OWN, 8),),
    ((OWN, 4),),
    (),
    ((DIAGONAL, 8), (OWN, 9), (LINES, 8),),
    ((DIAGONAL, 4),),
    ((LINES, 4), (OWN, 5),),
    ((SHARDS, 8), (DIAGONAL, 9),),
    ((LINES, 9), (OWN, 10),),
    ((DIAGONAL, 5),),
    ((LINES, 5), (OWN, 6),),
    ((SHARDS, 4), (DIAGONAL, 10),),
    ((OWN, 11),),
    ((DIAGONAL, 6),),
    ((OWN, 7), (SHARDS, 9),),
    ((LINES, 10), (DONE, 8), (DONE, 4),),
    ((DIAGONAL, 11),),
    (),
    (),
    ((SHARDS, 5), (DIAGONAL, 7), (LINES, 6), (OWN, 3),),
    ((DONE, 9),),
    ((LINES, 11), (DONE, 5),),
    ((LINES, 7), (OWN, 2), (DONE, 10), (DIAGONAL, 3),),
    ((DONE, 6),),
    ((DIAGONAL, 2),),
    ((OWN, 1), (DONE, 11), (LINES, 3),),
    ((LINES, 2), (DONE, 7),),
    ((DIAGONAL, 1),),
    ((OWN, 0), (DONE, 3),),
    ((LINES, 1),),
    ((DIAGONAL, 0), (DONE, 2),),
    ((DONE, 1), (LINES, 0), (DONE, 0),),
)


def nn(left, right):
    return lax.dot_general(left, right, (((1,), (0,)), ((), ())), preferred_element_type=f32)


def nt(left, right):
    return lax.dot_general(left, right, (((1,), (1,)), ((), ())), preferred_element_type=f32)


def tn(left, right):
    return lax.dot_general(left, right, (((0,), (0,)), ((), ())), preferred_element_type=f32)


def tile(index, size):
    if isinstance(index, int):
        return pl.ds(index * size, size)
    return pl.ds(pl.multiple_of(index * size, size), size)


def loop(count, body):
    def step(index, carry):
        body(index)
        return carry

    if count == 1:
        body(0)
    else:
        lax.fori_loop(0, count, step, 0)


def mean_last(values):
    return jnp.sum(values, axis=-1, keepdims=True) * (1.0 / values.shape[-1])


def fold_rows(values):
    return jnp.sum(values.reshape(values.shape[0] // 8, 8, values.shape[1]), axis=0)


def fold_tile(values):
    folded = fold_rows(values)
    return sum(folded[:, c : c + LANES] for c in range(0, folded.shape[1], LANES))


def unit_part(refs, u):
    if u < 3:
        return jnp.concatenate([refs[0][k, :, pl.ds(u * LANES, LANES)] for k in range(3)], axis=1)
    if u == 3:
        return refs[1][...]
    return refs[2 + (u - 4) // 4][:, pl.ds((u % 4) * HALF, HALF)]


def adam_moments(gradient, first_moment, second_moment):
    first_new = BETA_FIRST * first_moment + (1.0 - BETA_FIRST) * gradient
    second_new = BETA_SECOND * second_moment + (1.0 - BETA_SECOND) * gradient * gradient
    direction = (
        first_new
        / (1.0 - BETA_FIRST**STEP)
        / (jnp.sqrt(second_new / (1.0 - BETA_SECOND**STEP)) + ADAM_EPS)
    )
    return (first_new, second_new, direction)


def head_lane():
    return lax.broadcasted_iota(jnp.int32, (1, QUAD), 1) // HEAD


def spread_heads(values):
    lane = head_lane()
    zero = jnp.zeros_like(values)
    return jnp.concatenate([jnp.where(lane == head, values, zero) for head in range(4)], axis=0)


def pick_heads(values, length):
    lane = head_lane()
    result = values[:length]
    for head in range(1, 4):
        result = jnp.where(lane == head, values[head * length : (head + 1) * length], result)
    return result


def lanes(offset, size=LANES):
    if isinstance(offset, int):
        return pl.ds(offset, size)
    return pl.ds(pl.multiple_of(offset, LANES), size)


def pair(ref, rows, offset):
    return jnp.concatenate([ref[rows, lanes(offset)], ref[rows, lanes(HALF + offset)]], axis=1)


def put_pair(ref, rows, offset, values):
    ref[rows, lanes(offset)] = values[:, :LANES]
    ref[rows, lanes(HALF + offset)] = values[:, LANES:]


def main_kernel(
    comm,
    lengths,
    tokens_hbm,
    cot_hbm,
    small,
    w_in,
    w_mid,
    w_up,
    w_down,
    *rest,
):
    if comm:
        *moments_hbm, out_hbm, back_hbm, shard, vectors, norms, probs_hbm = rest[:14]
        rest = rest[14:]
    else:
        whole_hbm, out_hbm, back_hbm, shard, vectors, probs_hbm = rest[:6]
        rest = rest[6:]
    (
        back,
        unit,
        packed,
        context,
        normed,
        inverse,
        first,
        hidden,
        slope,
        own,
        cot,
        flip_a,
        flip_b,
        probs,
        sums,
        up_sums,
        local_sem,
        probs_sem,
        *rest,
    ) = rest
    if comm:
        sib_in, diag_in, line_in, z_in, *rest = rest
        squares, square_in, vec_sum, vec_in, vec_z_in = rest[:5]
        send, recv, rs_send, rs_recv, vec_send, vec_recv, square_send, square_recv, held_sem, shard_sem = rest[5:]
    micro, per_micro = lengths.shape
    chains = micro * per_micro
    length = own.shape[0] // chains
    count = own.shape[0]

    planes = unit.shape[1]
    if comm:
        rank = lax.axis_index("dp")
        core = lax.axis_index("mp")
        z, y, x = rank // 4, (rank // 2) % 2, rank % 2
        mine = pl.ds(pl.multiple_of(core * HALF, HALF), HALF)
        other = pl.ds(pl.multiple_of((1 - core) * HALF, HALF), HALF)

        def device(zz, yy, xx, cc):
            return (zz * 4 + yy * 2 + xx, cc)

        y1, x1 = jnp.where(core == 0, y, 1 - y), jnp.where(core == 0, 1 - x, x)
        y2, x2 = jnp.where(core == 0, 1 - y, y), jnp.where(core == 0, x, 1 - x)
        near = device(z, y1, x1, core)
        next_ = device(z, y2, x2, core)
        sibling = device(z, y, x, 1 - core)

        def plane(step):
            return lax.rem(z + step, planes)

        def plane_back(step):
            return lax.rem(z + planes - step, planes)

        def remote(src, dst, ssem, rsem, target):
            return pltpu.make_async_remote_copy(
                src_ref=src,
                dst_ref=dst,
                send_sem=ssem,
                recv_sem=rsem,
                device_id=target,
                device_id_type=MESH,
            )

        LINE = planes - 1

        def gz(u, step):
            piece = unit.at[u, z, y, x, :, mine]
            return remote(
                piece, piece, send.at[u, step - 1], recv.at[u, step - 1], device(plane(step), y, x, core)
            )

        def gline(u, which):
            piece = unit.at[u, :, y, x, :, mine]
            return remote(
                piece,
                piece,
                send.at[u, LINE + which],
                recv.at[u, LINE + which],
                near if which else next_,
            )

        def gdiag(u):
            piece = unit.at[u, :, y2, x2, :, mine]
            return remote(piece, piece, send.at[u, LINE + 2], recv.at[u, LINE + 2], near)

        def gsib(u):
            piece = unit.at[u, :, :, :, :, mine]
            return remote(piece, piece, send.at[u, LINE + 3], recv.at[u, LINE + 3], sibling)

        def gshard(u):
            piece = unit.at[u, z, y, x, :, mine]
            return remote(piece, piece, send.at[u, LINE], recv.at[u, LINE], next_)

        def gz_next(u, step):
            piece = unit.at[u, z, y2, x2, :, mine]
            sem = LINE + 3 + step
            return remote(piece, piece, send.at[u, sem], recv.at[u, sem], device(plane(step), y, x, core))

        def ag_z(u):
            for step in range(1, planes):
                gz(u, step).start()
            if u in SPLIT_GATHER:
                gshard(u).start()

        def ag_shard(u):
            gshard(u).wait_recv()
            for step in range(1, planes):
                gz_next(u, step).start()

        def ag_line(u):
            for step in range(1, planes):
                gz(u, step).wait_recv()
            if u not in SPLIT_GATHER:
                gline(u, 0).start()
            gline(u, 1).start()

        def ag_diag(u):
            if u in SPLIT_GATHER:
                for step in range(1, planes):
                    gz_next(u, step).wait_recv()
            else:
                gline(u, 0).wait_recv()
            gdiag(u).start()

        def ag_sib(u):
            gline(u, 1).wait_recv()
            gdiag(u).wait_recv()
            gsib(u).start()

        def ag_ready(u):
            gsib(u).wait_recv()

        def ag_sent(u):
            for step in range(1, planes):
                gz(u, step).wait_send()
            if u in SPLIT_GATHER:
                gshard(u).wait_send()
                for step in range(1, planes):
                    gz_next(u, step).wait_send()
            else:
                gline(u, 0).wait_send()
            gline(u, 1).wait_send()
            gdiag(u).wait_send()
            gsib(u).wait_send()

        def slot(u):
            return G_SLOT.get(u, u)

        def rsib(u, place=None):
            place = slot(u) if place is None else place
            return remote(
                unit.at[place, :, :, :, :, other], sib_in.at[u], rs_send.at[u, 0], rs_recv.at[u, 0], sibling
            )

        def rdiag(u):
            return remote(
                unit.at[slot(u), :, 1 - y, 1 - x, :, mine],
                diag_in.at[u],
                rs_send.at[u, 1],
                rs_recv.at[u, 1],
                near,
            )

        def rline(u, which):
            yy, xx = (y2, x2) if which else (y1, x1)
            return remote(
                unit.at[slot(u), :, yy, xx, :, mine],
                line_in.at[u, which],
                rs_send.at[u, 2 + which],
                rs_recv.at[u, 2 + which],
                next_ if which else near,
            )

        def rz(u, step):
            return remote(
                unit.at[slot(u), plane(step), y, x, :, mine],
                z_in.at[u, step - 1],
                rs_send.at[u, 3 + step],
                rs_recv.at[u, 3 + step],
                device(plane(step), y, x, core),
            )

        def rz_next(u, step):
            sem = 3 + planes + step - 1
            return remote(
                unit.at[slot(u), plane(step), y2, x2, :, mine],
                line_in.at[u, 1, step - 1],
                rs_send.at[u, sem],
                rs_recv.at[u, sem],
                device(plane(step), y, x, core),
            )

        def rshard(u):
            return remote(
                unit.at[slot(u), z, y2, x2, :, mine],
                line_in.at[u, 1, planes - 1],
                rs_send.at[u, 3],
                rs_recv.at[u, 3],
                next_,
            )

        def rs_start(u, place=None):
            rsib(u, place).start()

        def rs_own(u):
            rsib(u).wait_recv()

            def add(zz):
                for yy in range(2):
                    for xx in range(2):
                        unit[slot(u), zz, yy, xx, :, mine] = (
                            unit[slot(u), zz, yy, xx, :, mine].astype(f32) + sib_in[u, zz, yy, xx].astype(f32)
                        ).astype(bf16)

            loop(planes, add)
            rdiag(u).start()
            rline(u, 0).start()

        def rs_diag(u):
            rdiag(u).wait_recv()

            def add(zz):
                unit[slot(u), zz, y2, x2, :, mine] = (
                    unit[slot(u), zz, y2, x2, :, mine].astype(f32) + diag_in[u, zz].astype(f32)
                ).astype(bf16)

            loop(planes, add)
            if u in SPLIT_SUMS:
                for step in range(1, planes):
                    rz_next(u, step).start()
            else:
                rline(u, 1).start()

        def rs_shard(u):
            total = unit[slot(u), z, y2, x2, :, mine].astype(f32)
            for step in range(1, planes):
                rz_next(u, step).wait_recv()
                total = total + line_in[u, 1, step - 1].astype(f32)
            unit[slot(u), z, y2, x2, :, mine] = total.astype(bf16)
            rshard(u).start()

        def rs_line(u):
            rline(u, 0).wait_recv()
            if u not in SPLIT_SUMS:
                rline(u, 1).wait_recv()

            def add(zz):
                total = unit[slot(u), zz, y, x, :, mine].astype(f32) + line_in[u, 0, zz].astype(f32)
                if u not in SPLIT_SUMS:
                    total = total + line_in[u, 1, zz].astype(f32)
                unit[slot(u), zz, y, x, :, mine] = total.astype(bf16)

            loop(planes, add)
            for step in range(1, planes):
                rz(u, step).start()

        def rs_done(u):
            total = unit[slot(u), z, y, x, :, mine].astype(f32)
            for step in range(1, planes):
                rz(u, step).wait_recv()
                total = total + z_in[u, step - 1].astype(f32)
            if u in SPLIT_SUMS:
                rshard(u).wait_recv()
                total = total + line_in[u, 1, planes - 1].astype(f32)
            _, _, direction = adam_moments(total, normed[held(0, u)], normed[held(1, u)])
            weight = normed[held(2, u)]
            normed[held(0, u)] = total
            shard_copy(u).start()
            heading = direction + DECAY_RATE * weight
            which = MATRIX_OF[u]
            squares[which] += fold_tile(weight * weight)
            squares[4 + which] += fold_tile(heading * heading)

        def held(which, u):
            rows = normed.shape[0] // 20
            row = (which * UNITS + u) // 2 * rows
            return pl.ds(row, rows), pl.ds((u % 2) * HALF, HALF)

        def held_copies(which):
            matrices = (moments_hbm[:4], moments_hbm[4:], (w_in, w_mid, w_up, w_down))[which]
            copies = []
            for u in range(UNITS):
                rows, cols = held(which, u)
                if u < 3:
                    pairs = [
                        (
                            matrices[0].at[k, :, pl.ds(u * LANES, LANES)],
                            normed.at[rows, pl.ds(cols.start + k * LANES, LANES)],
                        )
                        for k in range(3)
                    ]
                elif u == 3:
                    pairs = [(matrices[1], normed.at[rows, cols])]
                else:
                    piece = matrices[2 + (u - 4) // 4].at[:, pl.ds((u % 4) * HALF, HALF)]
                    pairs = [(piece, normed.at[rows, cols])]
                for source, target in pairs:
                    sem = held_sem.at[which, len(copies)]
                    copies.append(pltpu.make_async_copy(source, target, sem))
            return copies

        def shard_copy(u):
            return pltpu.make_async_copy(normed.at[held(0, u)], shard.at[u], shard_sem.at[u])

        def rs_sent(u):
            rsib(u).wait_send()
            rdiag(u).wait_send()
            rline(u, 0).wait_send()
            if u in SPLIT_SUMS:
                rshard(u).wait_send()
                for step in range(1, planes):
                    rz_next(u, step).wait_send()
            else:
                rline(u, 1).wait_send()
            for step in range(1, planes):
                rz(u, step).wait_send()

    if comm:
        gathers = {
            PLANES: ag_z,
            SHARDS: ag_shard,
            LINES: ag_line,
            DIAGONAL: ag_diag,
            SIBLING: ag_sib,
        }
        sums_of = {
            OWN: rs_own,
            DIAGONAL: rs_diag,
            SHARDS: rs_shard,
            LINES: rs_line,
            DONE: rs_done,
        }
    gather_plan, reduce_plan = iter(GATHER), iter(REDUCE)

    def planned(plan, kinds):
        def run():
            for kind, u in next(plan):
                if comm:
                    kinds[kind](u)

        return run

    kinds = (gathers, sums_of) if comm else ({}, {})
    gather, reduce = planned(gather_plan, kinds[0]), planned(reduce_plan, kinds[1])

    def staged(plan, turns, stages, extra=None):
        sends = [[next(plan) for _ in stages] for _ in range(turns)]
        kinds_here = kinds[0] if plan is gather_plan else kinds[1]

        def turn(i):
            for s, stage in enumerate(stages):
                stage(i)
                for k in range(turns):
                    more = extra.get((k, s)) if extra else None
                    if comm and (sends[k][s] or more):

                        @pl.when(i == k)
                        def _(k=k, s=s, more=more):
                            for kind, u in sends[k][s]:
                                kinds_here[kind](u)
                            if more:
                                more()

        loop(turns, turn)

    def nothing(i):
        pass

    def ready(u):
        if comm:
            ag_ready(u)

    def weights(u):
        return unit[u].reshape(WIDE, WIDE)

    def unit_cols(u, columns):
        return unit[u, :, :, :, :, columns].reshape(WIDE, columns.size)

    own_copy = pltpu.make_async_copy(tokens_hbm, own, local_sem.at[0])
    cot_copy = pltpu.make_async_copy(cot_hbm, cot, local_sem.at[1])
    out_copy = pltpu.make_async_copy(cot, out_hbm, local_sem.at[2])
    back_copy = pltpu.make_async_copy(back, back_hbm, local_sem.at[3])
    if comm:
        weight_copies = held_copies(2)
        for copy in weight_copies:
            copy.start()
    own_copy.start()
    cot_copy.start()

    if comm:
        barrier = pltpu.get_barrier_semaphore()
        around = [
            device(z, yy, xx, cc)
            for yy, xx, cc in (
                (y, x, 1 - core),
                (y, 1 - x, core),
                (1 - y, x, core),
                (1 - y, 1 - x, core),
                (y, 1 - x, 1 - core),
                (1 - y, x, 1 - core),
                (1 - y, 1 - x, 1 - core),
            )
        ]
        greeted = around + [device(plane(step), y, x, core) for step in range(1, planes)]
        for target in greeted:
            pl.semaphore_signal(barrier, inc=1, device_id=target, device_id_type=MESH)
        for copy in weight_copies:
            copy.wait()
        for u in range(UNITS):
            unit[u, z, y, x, :, mine] = normed[held(2, u)].astype(bf16)
        pl.semaphore_wait(barrier, len(greeted))
    else:
        unit_copy = pltpu.make_async_copy(whole_hbm, unit, local_sem.at[4])
        unit_copy.start()
        unit_copy.wait()

    gather()
    sums[...] = jnp.zeros_like(sums)
    up_sums[...] = jnp.zeros_like(up_sums)
    if comm:
        squares[...] = jnp.zeros_like(squares)
    own_copy.wait()
    cot_copy.wait()

    def shift_sums(r):
        sums[7] += fold_rows(cot[tile(r, BLOCK), :].astype(f32))

    loop(count // BLOCK, shift_sums)

    def fold_vectors():
        target = vec_sum.at[0] if comm else vectors
        target[pl.ds(0, 8), :] = jnp.sum(sums[...], axis=1)
        folded = jnp.sum(up_sums[...], axis=1)
        for u in range(4):
            for c in range(2):
                target[pl.ds(8 + c * 2 + u // 2, 1), pl.ds((u % 2) * HALF, HALF)] = folded[
                    u : u + 1, c * HALF : (c + 1) * HALF
                ]

    if comm:
        place = (y * 2 + x) * 2 + core
        vec_targets = (sibling, device(z, y, 1 - x, core), device(z, 1 - y, x, core))

        def vec_copy(stage):
            return remote(
                vec_sum.at[stage],
                vec_in.at[stage],
                vec_send.at[stage],
                vec_recv.at[stage],
                vec_targets[stage],
            )

        def vec_plane(step):
            return remote(
                vec_sum.at[3],
                vec_z_in.at[z],
                vec_send.at[2 + step],
                vec_recv.at[2 + step],
                device(plane(step), y, x, core),
            )

        def vec_start():
            vec_copy(0).start()

        def vec_step(stage):
            vec_copy(stage).wait_recv()
            vec_sum[stage + 1] = vec_sum[stage] + vec_in[stage]
            if stage < 2:
                vec_copy(stage + 1).start()
            else:
                vec_z_in[z] = vec_sum[3]
                for step in range(1, planes):
                    vec_plane(step).start()

        def vec_done():
            for step in range(1, planes):
                vec_plane(step).wait_recv()
            total = vec_z_in[0]
            for zz in range(1, planes):
                total = total + vec_z_in[zz]
            vectors[...] = total

        def vec_sent():
            for stage in range(3):
                vec_copy(stage).wait_send()
            for step in range(1, planes):
                vec_plane(step).wait_send()

        def square_near(step):
            piece = square_in.at[place]
            return remote(piece, piece, square_send.at[step], square_recv.at[step], around[step])

        def square_far(step):
            piece = square_in.at[8 + z]
            sem = len(around) - 1 + step
            return remote(
                piece, piece, square_send.at[sem], square_recv.at[sem], device(plane(step), y, x, core)
            )

        def exchange_squares():
            square_in[place] = jnp.sum(squares[...], axis=1)
            for step in range(len(around)):
                square_near(step).start()
            for step in range(len(around)):
                square_near(step).wait_recv()
            square_in[8 + z] = jnp.sum(square_in[pl.ds(0, 8)], axis=0)
            for step in range(1, planes):
                square_far(step).start()
            for step in range(1, planes):
                square_far(step).wait_recv()
            total = jnp.sum(square_in[pl.ds(8, planes)], axis=0)
            norms[...] = jnp.broadcast_to(
                jnp.sqrt(jnp.sum(total, axis=1, keepdims=True)), norms.shape
            )
            for step in range(len(around)):
                square_near(step).wait_send()
            for step in range(1, planes):
                square_far(step).wait_send()

    def probs_out(t, chain):
        return pltpu.make_async_copy(probs.at[chain], probs_hbm.at[t], probs_sem.at[chain])

    def probs_back(t, chain):
        return pltpu.make_async_copy(probs_hbm.at[t], probs.at[chain], probs_sem.at[chain])

    position = lax.broadcasted_iota(jnp.int32, (1, length), 1)

    def project(g):
        ready(g)
        bias = jnp.concatenate(
            [
                piece
                for c in range(2)
                for piece in (
                    small[pl.ds(0, 1), lanes(c * HALF + g * LANES)],
                    jnp.zeros((1, LANES), f32),
                    small[pl.ds(1, 1), lanes(c * HALF + g * LANES)],
                )
            ],
            axis=1,
        )
        lane = lax.broadcasted_iota(jnp.int32, (1, WIDE), 1) % HALF
        scale = jnp.where(lane < LANES, HEAD ** (-0.5), 1.0)
        for j in range(3):
            cols = pl.ds(j * QUAD, QUAD)
            part = slice(j * QUAD, (j + 1) * QUAD)
            packed[g, :, cols] = (
                (nn(own[...], unit_cols(g, cols)) + bias[:, part]).astype(bf16).astype(f32)
                * scale[:, part]
            ).astype(bf16)

    def attend(g, chain):
        rows = pl.ds(chain * length, length)
        here = packed.at[g]
        queries = spread_heads(pair(here, rows, 0))
        keys = pair(here, rows, LANES)
        values = pair(here, rows, 2 * LANES)
        limit = lengths[chain // per_micro, chain % per_micro]
        scores = jnp.where(position < limit, nt(queries, keys), MASKED_SCORE)
        peak = jnp.max(scores, axis=1, keepdims=True)
        exponent = jnp.exp(scores - peak)
        total = jnp.sum(exponent, axis=1, keepdims=True)
        low = (exponent * (1.0 / total)).astype(bf16)
        mixed = pick_heads(nn(low, values), length).astype(bf16)
        return rows, low, mixed

    def attend_some(some):
        def stage(g):
            @pl.when(g > 0)
            def _():
                for chain in some:
                    probs_out((g - 1) * chains + chain, chain).wait()

            for chain, (rows, low, mixed) in [(chain, attend(g, chain)) for chain in some]:
                probs[chain, :, pl.ds(0, length)] = low
                put_pair(context, rows, g * LANES, mixed)

            @pl.when(g < 2)
            def _():
                for chain in some:
                    probs_out(g * chains + chain, chain).start()

        return stage

    halves = (range(chains // 2), range(chains // 2, chains))
    staged(gather_plan, 3, [nothing, project] + [attend_some(some) for some in halves])

    gather()
    ready(3)

    def mid(r):
        rows = tile(r, count)
        back[rows, :] = nt(context[rows, :], weights(3))

    loop(1, mid)
    gather()

    def first_norm(r):
        rows = tile(r, BLOCK)
        value = own[rows, :].astype(f32) + back[rows, :] + small[pl.ds(2, 1), :]
        center = value - mean_last(value)
        root = lax.rsqrt(mean_last(center * center) + NORM_EPS)
        scaled = center * root
        normed[rows, :] = scaled
        inverse[rows, :] = root
        shifted = scaled * small[pl.ds(3, 1), :] + small[pl.ds(4, 1), :]
        first[rows, :] = shifted.astype(bf16)
        back[rows, :] = shifted + small[pl.ds(5, 1), :]

    loop(count // BLOCK, first_norm)
    gather()

    def up(u):
        ready(4 + u)
        bias = jnp.concatenate(
            [
                small[pl.ds(8 + c * 2 + u // 2, 1), lanes((u % 2) * HALF, HALF)]
                for c in range(2)
            ],
            axis=1,
        )
        for j in range(3):
            cols = pl.ds(j * QUAD, QUAD)
            upper = nn(first[...], unit_cols(4 + u, cols)) + bias[:, j * QUAD : (j + 1) * QUAD]
            share = 0.5 + 0.5 * lax.erf(upper * 0.7071067811865476)
            hidden[u, :, cols] = (upper * share).astype(bf16)
            slope[u, :, cols] = (
                share + upper * (0.3989422804014327 * jnp.exp(-0.5 * upper * upper))
            ).astype(bf16)

    def down(u):
        ready(8 + u)
        back[...] += nt(hidden[u], weights(8 + u))

    staged(gather_plan, 4, [nothing, up])
    staged(gather_plan, 4, [nothing, down])
    if comm:
        for u in range(UNITS):
            ag_sent(u)
    def flip(source, target):
        for j in range(WIDE // LANES):
            cols = pl.ds(j * LANES, LANES)
            target[cols, :] = source[:, cols].T

    def second_norm(r):
        rows = tile(r, BLOCK)
        value = back[rows, :]
        center = value - mean_last(value)
        root = lax.rsqrt(mean_last(center * center) + NORM_EPS)
        scaled = center * root
        upstream = cot[rows, :].astype(f32)
        cot[rows, :] = (scaled * small[pl.ds(6, 1), :] + small[pl.ds(7, 1), :]).astype(bf16)
        gained = upstream * small[pl.ds(6, 1), :]
        grad = (gained - mean_last(gained) - scaled * mean_last(gained * scaled)) * root
        back[rows, :] = grad
        low = grad.astype(bf16)
        own[rows, :] = low
        sums[5] += fold_rows(low.astype(f32))
        sums[6] += fold_rows(upstream * scaled)

    loop(count // BLOCK, second_norm)
    out_copy.start()
    flip(own, flip_a)
    flip(first, flip_b)

    def outer(place, flipped, source):
        part = nn(flipped[...], source[...]).astype(bf16)
        unit[place] = part.reshape(unit.shape[1:])

    def hidden_back(u):
        for j in range(3):
            cols = pl.ds(j * QUAD, QUAD)
            low = (nn(own[...], unit_cols(8 + u, cols)) * slope[u, :, cols].astype(f32)).astype(bf16)
            slope[u, :, cols] = low
            up_sums[u, :, cols] += fold_rows(low.astype(f32))

    def down_sums(u):
        outer(8 + u, flip_a, hidden.at[u])
        if comm:
            rs_start(8 + u, 8 + u)

    def first_part(u):
        back[...] += nt(slope[u], weights(4 + u))

    def up_sums_out(u):
        outer(4 + u, flip_b, slope.at[u])
        if comm:
            rs_start(4 + u, 4 + u)

    staged(reduce_plan, 4, [hidden_back, down_sums, first_part, up_sums_out])

    def first_back(r):
        rows = tile(r, BLOCK)
        upstream = back[rows, :]
        scaled = normed[rows, :]
        gained = upstream * small[pl.ds(3, 1), :]
        grad = (gained - mean_last(gained) - scaled * mean_last(gained * scaled)) * inverse[rows, :]
        back[rows, :] = grad
        low = grad.astype(bf16)
        own[rows, :] = low
        sums[2] += fold_rows(low.astype(f32))
        sums[3] += fold_rows(upstream * scaled)
        sums[4] += fold_rows(upstream)

    loop(count // BLOCK, first_back)
    if comm:
        step_copies = held_copies(0) + held_copies(1) + held_copies(2)
        for copy in step_copies:
            copy.start()
    reduce()
    out_copy.wait()
    flip(own, flip_a)
    if comm:
        for copy in step_copies:
            copy.wait()
    reduce()

    for j in range(3):
        cols = pl.ds(j * QUAD, QUAD)
        cot[:, cols] = nn(own[...], unit_cols(3, cols)).astype(bf16)
    reduce()
    outer(3, flip_a, context)
    if comm:
        rs_start(3)
    own_again = pltpu.make_async_copy(tokens_hbm, own, local_sem.at[0])
    own_again.start()
    reduce()
    own_again.wait()
    flip(own, flip_b)
    reduce()

    def attend_back(g, chain):
        rows = pl.ds(chain * length, length)
        here = packed.at[g]
        queries = spread_heads(pair(here, rows, 0))
        keys = pair(here, rows, LANES)
        values = pair(here, rows, 2 * LANES)
        d_context = spread_heads(pair(cot, rows, g * LANES))
        low = probs[chain, :, pl.ds(0, length)]
        wide = low.astype(f32)
        d_probs = nt(d_context, values)
        inner = jnp.sum(wide * d_probs, axis=1, keepdims=True)
        d_scores = (wide * (d_probs - inner)).astype(bf16)
        d_queries = (pick_heads(nn(d_scores, keys), length) * HEAD ** (-0.5)).astype(bf16)
        d_keys = tn(d_scores, queries).astype(bf16)
        d_values = tn(low, d_context).astype(bf16)
        return rows, d_queries, d_keys, d_values

    def back_some(some):
        def stage(i):
            g = 2 - i
            grads = hidden.at[g]

            @pl.when(g < 2)
            def _():
                for chain in some:
                    probs_back(g * chains + chain, chain).wait()

            results = [attend_back(g, chain) for chain in some]
            for rows, d_queries, d_keys, d_values in results:
                put_pair(grads, rows, 0, d_queries)
                put_pair(grads, rows, LANES, d_keys)
                put_pair(grads, rows, 2 * LANES, d_values)
            for row, place_of in ((0, 1), (1, 3)):
                folded = sum(fold_rows(result[place_of].astype(f32)) for result in results)
                for c in range(2):
                    cols = lanes(c * HALF + g * LANES)
                    sums[row, :, cols] += folded[:, c * LANES : (c + 1) * LANES]

            @pl.when(g > 0)
            def _():
                for chain in some:
                    probs_back((g - 1) * chains + chain, chain).start()

        return stage

    def head_sums(i):
        g = 2 - i
        place = 8 + (i + 1) % 3
        outer(place, flip_b, hidden.at[g])
        if comm:
            rs_start(g, place)

    def vectors_out():
        fold_vectors()
        vec_start()

    def freed(k):
        def run():
            rs_sent(G_SLOT[2 - k])
            if k == 2:
                vectors_out()

        return run

    def tokens_back(i):
        g = 2 - i
        back[...] += nt(hidden[g], weights(g))

    def tokens_out():
        back_copy.start()
        vec_step(2)

    staged(
        reduce_plan,
        3,
        [back_some(some) for some in halves] + [head_sums],
        {(k, 1): freed(k) for k in range(3)} if comm else None,
    )
    staged(
        reduce_plan,
        3,
        [tokens_back],
        {(0, 0): lambda: vec_step(0), (1, 0): lambda: vec_step(1), (2, 0): tokens_out}
        if comm
        else None,
    )
    if not comm:
        fold_vectors()
        back_copy.start()

    if comm:
        reduce()
        vec_done()
        exchange_squares()
        for u in range(UNITS):
            if u not in G_SLOT.values():
                rs_sent(u)
            shard_copy(u).wait()
        vec_sent()
    else:
        whole_out = pltpu.make_async_copy(unit, shard, local_sem.at[4])
        whole_out.start()
        whole_out.wait()
    back_copy.wait()


def run_layer(tokens, lengths, cotangent, weights, moments, small, ranks):
    rows_here = weights[1].shape[0]
    width = small.shape[1]
    flat = tokens.reshape(-1, width)
    count = flat.shape[0]
    chains = lengths.size
    length = tokens.shape[2]
    comm = gathers_inside(ranks, rows_here)
    planes = ranks // 4 if comm else 4
    padded = -(-length // LANES) * LANES
    steps = planes - 1
    unit_shape = (UNITS, planes, 2, 2, width // (planes * 4), WIDE)
    vmem = pl.BlockSpec(memory_space=pltpu.VMEM)
    hbm = pl.BlockSpec(memory_space=pl.ANY)
    operands = [lengths, flat, cotangent.reshape(-1, width), small, *weights]
    in_specs = [pl.BlockSpec(memory_space=pltpu.SMEM), hbm, hbm, vmem] + [hbm] * 4
    if not comm:
        shard = jnp.stack([unit_part(weights, u) for u in range(UNITS)]).astype(bf16)
        whole = lax.all_gather(shard, "dp", axis=1, tiled=True)
        whole = lax.all_gather(whole, "mp", axis=2, tiled=True)
        operands.append(whole.reshape(unit_shape))
        in_specs.append(hbm)
    else:
        operands += moments
        in_specs += [hbm] * 8
    shard_shape = (UNITS, rows_here, HALF)
    out_shape = [
        jax.ShapeDtypeStruct((count, width), bf16),
        jax.ShapeDtypeStruct((count, width), f32),
        jax.ShapeDtypeStruct(shard_shape, f32) if comm else jax.ShapeDtypeStruct(unit_shape, bf16),
        jax.ShapeDtypeStruct(small.shape, f32),
        jax.ShapeDtypeStruct((2 * chains, 4 * length, padded), bf16),
    ]
    out_specs = [hbm, hbm, hbm, vmem, hbm]
    if comm:
        out_shape.insert(4, jax.ShapeDtypeStruct((8, LANES), f32))
        out_specs.insert(4, vmem)
    scratch = [
        pltpu.VMEM((count, width), f32),
        pltpu.VMEM(unit_shape, bf16),
        pltpu.VMEM((3, count, WIDE), bf16),
        pltpu.VMEM((count, width), bf16),
        pltpu.VMEM((count, width), f32),
        pltpu.VMEM((count, 1), f32),
        pltpu.VMEM((count, width), bf16),
        pltpu.VMEM((4, count, WIDE), bf16),
        pltpu.VMEM((4, count, WIDE), bf16),
        pltpu.VMEM((count, width), bf16),
        pltpu.VMEM((count, width), bf16),
        pltpu.VMEM((width, count), bf16),
        pltpu.VMEM((width, count), bf16),
        pltpu.VMEM((chains, 4 * length, padded), bf16),
        pltpu.VMEM((8, 8, width), f32),
        pltpu.VMEM((4, 8, WIDE), f32),
        pltpu.SemaphoreType.DMA((5,)),
        pltpu.SemaphoreType.DMA((chains,)),
    ]
    params = dict(vmem_limit_bytes=64 * 2**20 - 2**16)
    if comm:
        scratch += [
            pltpu.VMEM((UNITS, planes, 2, 2, rows_here, HALF), bf16),
            pltpu.VMEM((UNITS, planes, rows_here, HALF), bf16),
            pltpu.VMEM((UNITS, 2, planes, rows_here, HALF), bf16),
            pltpu.VMEM((UNITS, steps, rows_here, HALF), bf16),
            pltpu.VMEM((8, 8, LANES), f32),
            pltpu.VMEM((8 + planes, 8, LANES), f32),
            pltpu.VMEM((4,) + small.shape, f32),
            pltpu.VMEM((3,) + small.shape, f32),
            pltpu.VMEM((planes,) + small.shape, f32),
            pltpu.SemaphoreType.DMA((UNITS, 2 * steps + 4)),
            pltpu.SemaphoreType.DMA((UNITS, 2 * steps + 4)),
            pltpu.SemaphoreType.DMA((UNITS, 2 * steps + 4)),
            pltpu.SemaphoreType.DMA((UNITS, 2 * steps + 4)),
            pltpu.SemaphoreType.DMA((3 + steps,)),
            pltpu.SemaphoreType.DMA((3 + steps,)),
            pltpu.SemaphoreType.DMA((7 + steps,)),
            pltpu.SemaphoreType.DMA((7 + steps,)),
            pltpu.SemaphoreType.DMA((3, UNITS + 6)),
            pltpu.SemaphoreType.DMA((UNITS,)),
        ]
        params.update(collective_id=0, has_side_effects=True)
    out, back, shard, vectors, *rest = pl.pallas_call(
        functools.partial(main_kernel, comm),
        out_shape=out_shape,
        in_specs=in_specs,
        out_specs=out_specs,
        scratch_shapes=scratch,
        compiler_params=pltpu.CompilerParams(**params),
    )(*operands)
    norms = rest[0] if comm else None
    if not comm:
        summed = shard.reshape(UNITS, width, 2, HALF).astype(f32)
        summed = lax.psum_scatter(summed, "mp", scatter_dimension=2, tiled=True)
        summed = lax.psum_scatter(
            summed.reshape(UNITS, width, HALF), "dp", scatter_dimension=1, tiled=True
        )
        shard = summed
    return out, back, shard, vectors, norms


def gathers_inside(ranks, rows_here):
    return ranks % 4 == 0 and rows_here % 16 == 0


def put_unit(refs, u, values):
    if u < 3:
        for k in range(3):
            refs[0][k, :, pl.ds(u * LANES, LANES)] = values[:, k * LANES : (k + 1) * LANES]
    elif u == 3:
        refs[1][...] = values
    else:
        refs[2 + (u - 4) // 4][:, pl.ds((u % 4) * HALF, HALF)] = values


def step_kernel(*refs):
    out_in, back_in, shard, vectors, norms = refs[:5]
    weights, moments = refs[5:9], refs[9:17]
    small, small_first, small_second = refs[17:20]
    outs = refs[20:-3]
    out_held, back_held, sem = refs[-3:]
    inward = [
        pltpu.make_async_copy(out_in, out_held, sem.at[0]),
        pltpu.make_async_copy(back_in, back_held, sem.at[1]),
    ]
    outward = [
        pltpu.make_async_copy(out_held, outs[0], sem.at[2]),
        pltpu.make_async_copy(back_held, outs[1], sem.at[3]),
    ]
    for copy in inward:
        copy.start()
    grads, firsts, seconds, news, lows = (
        [outs[2 + 5 * m + which] for m in range(4)] for which in range(5)
    )
    for u in range(UNITS):
        if u in (4, 8):
            inward[u // 4 - 1].wait()
            outward[u // 4 - 1].start()
        gradient = shard[u]
        first_new, second_new, direction = adam_moments(
            gradient, unit_part(moments[:4], u), unit_part(moments[4:], u)
        )
        weight = unit_part(weights, u)
        which = MATRIX_OF[u]
        rate = RATE_MATRIX * (norms[which : which + 1, :1] / norms[4 + which : 5 + which, :1])
        renewed = weight - rate * (direction + DECAY_RATE * weight)
        put_unit(grads, u, gradient)
        put_unit(firsts, u, first_new)
        put_unit(seconds, u, second_new)
        put_unit(news, u, renewed)
        put_unit(lows, u, renewed.astype(bf16))
    vector_grad = vectors[...]
    first_new, second_new, direction = adam_moments(vector_grad, small_first[...], small_second[...])
    outs[22][...] = vector_grad
    outs[23][...] = first_new
    outs[24][...] = second_new
    outs[25][...] = small[...] - RATE_VECTOR * direction
    for row in range(2):
        for m in range(4):
            outs[26][pl.ds(row, 1), pl.ds(m, 1)] = norms[4 * row + m : 4 * row + m + 1, :1]
    for copy in outward:
        copy.wait()


def run_step(out, back, shard, vectors, norms, weights, moments, small, small_first, small_second):
    vmem = pl.BlockSpec(memory_space=pltpu.VMEM)
    hbm = pl.BlockSpec(memory_space=pl.ANY)
    out_shape = [jax.ShapeDtypeStruct(out.shape, bf16), jax.ShapeDtypeStruct(back.shape, f32)]
    for weight in weights:
        out_shape += [jax.ShapeDtypeStruct(weight.shape, f32)] * 4
        out_shape += [jax.ShapeDtypeStruct(weight.shape, bf16)]
    out_shape += [jax.ShapeDtypeStruct(small.shape, f32)] * 4
    out_shape += [jax.ShapeDtypeStruct((2, 4), f32)]
    return pl.pallas_call(
        step_kernel,
        out_shape=out_shape,
        in_specs=[hbm, hbm] + [vmem] * 18,
        out_specs=[hbm, hbm] + [vmem] * 25,
        scratch_shapes=[
            pltpu.VMEM(out.shape, bf16),
            pltpu.VMEM(back.shape, f32),
            pltpu.SemaphoreType.DMA((4,)),
        ],
        compiler_params=pltpu.CompilerParams(vmem_limit_bytes=64 * 2**20 - 2**16),
    )(out, back, shard, vectors, norms, *weights, *moments, small, small_first, small_second)


def body(
    ranks,
    tokens,
    lengths,
    cotangent,
    attn_in,
    attn_out,
    ffn_in,
    ffn_out,
    attn_in_first,
    attn_in_second,
    attn_out_first,
    attn_out_second,
    ffn_in_first,
    ffn_in_second,
    ffn_out_first,
    ffn_out_second,
    small,
    small_first,
    small_second,
):
    weights = (attn_in.transpose(1, 0, 2), attn_out.T, ffn_in, ffn_out.T)
    all_moments = (
        attn_in_first.transpose(1, 0, 2),
        attn_out_first.T,
        ffn_in_first,
        ffn_out_first.T,
        attn_in_second.transpose(1, 0, 2),
        attn_out_second.T,
        ffn_in_second,
        ffn_out_second.T,
    )
    output, tokens_grad, shard, vectors, norms = run_layer(
        tokens, lengths, cotangent, weights, all_moments, small, ranks
    )
    if norms is not None:
        results = run_step(
            output,
            tokens_grad,
            shard,
            vectors,
            norms,
            weights,
            all_moments,
            small,
            small_first,
            small_second,
        )
        results = list(results)
        results[0] = results[0].reshape(tokens.shape)
        results[1] = results[1].reshape(tokens.shape)
        for i in range(5):
            results[2 + i] = results[2 + i].transpose(1, 0, 2)
            results[7 + i] = results[7 + i].T
            results[17 + i] = results[17 + i].T
        return tuple(results)
    output, tokens_grad = output.reshape(tokens.shape), tokens_grad.reshape(tokens.shape)
    rows = attn_in.shape[0]
    grad_in = jnp.concatenate([shard[g].reshape(rows, 3, LANES) for g in range(3)], axis=2)
    grad_mid = shard[3].T
    grad_up = jnp.concatenate([shard[4 + u] for u in range(4)], axis=1)
    grad_down = jnp.concatenate([shard[8 + u].T for u in range(4)], axis=0)
    matrices = (
        (attn_in, grad_in, attn_in_first, attn_in_second),
        (attn_out, grad_mid, attn_out_first, attn_out_second),
        (ffn_in, grad_up, ffn_in_first, ffn_in_second),
        (ffn_out, grad_down, ffn_out_first, ffn_out_second),
    )
    moments = [adam_moments(entry[1], entry[2], entry[3]) for entry in matrices]
    headings = [moments[i][2] + DECAY_RATE * matrices[i][0] for i in range(4)]
    weight_squares = jnp.stack([jnp.sum(entry[0] * entry[0]) for entry in matrices])
    step_squares = jnp.stack([jnp.sum(heading * heading) for heading in headings])
    vector_grad, weight_sums, step_sums = lax.psum(
        (vectors, weight_squares, step_squares), ("dp", "mp")
    )
    weight_norms = jnp.sqrt(weight_sums)
    step_norms = jnp.sqrt(step_sums)
    results = [output, tokens_grad]
    for i in range(4):
        weight = matrices[i][0]
        renewed = weight - RATE_MATRIX * (weight_norms[i] / step_norms[i]) * headings[i]
        results.extend(
            [matrices[i][1], moments[i][0], moments[i][1], renewed, renewed.astype(bf16)]
        )
    small_first_new, small_second_new, small_direction = adam_moments(
        vector_grad, small_first, small_second
    )
    small_new = small - RATE_VECTOR * small_direction
    results.extend(
        [
            vector_grad,
            small_first_new,
            small_second_new,
            small_new,
            jnp.stack((weight_norms, step_norms)),
        ]
    )
    return tuple(results)


def solution(mesh):
    chains = P(None, ("dp", "mp"), None, None)
    rows_three = P("dp", None, "mp")
    rows_two = P("dp", "mp")
    columns = P("mp", "dp")
    whole = P()
    return jax.shard_map(
        functools.partial(body, mesh.shape["dp"]),
        mesh=mesh,
        in_specs=(
            chains,
            P(None, ("dp", "mp")),
            chains,
            rows_three,
            columns,
            rows_two,
            columns,
            rows_three,
            rows_three,
            columns,
            columns,
            rows_two,
            rows_two,
            columns,
            columns,
            whole,
            whole,
            whole,
        ),
        out_specs=(
            (chains, chains)
            + (rows_three,) * 5
            + (columns,) * 5
            + (rows_two,) * 5
            + (columns,) * 5
            + (whole,) * 5
        ),
        check_vma=False,
    )
```
